256 devices in a mesh: tm: 8 (over y_hi, x), space: 32 (over z, y_lo, core).
Axes of the slice: x: 4, y: 4 (y_hi: 2, y_lo: 2; y = y_hi * 2 + y_lo), z: 8, core: 2. Of those that a mesh axis runs over, the one named last changes fastest.
Arguments:
- vectors: float32 [8, 2, 3, 64, 8192], P('tm', None, None, None, 'space'), may hold values from -6 to 6
- perambulators: float32 [8, 16, 2, 4096], P('tm'), may hold values from -0.75 to 0.75
- shift_steps: int32 [8], P('tm'), may hold values from 1 to 7, as said below
- spin_choice: int32 [4, 3], replicated, may hold values from 0 to 15
Outputs:
- elementals: float32 [8, 64, 2, 4096], P('tm', 'space')
- correlator: float32 [8, 4, 2], P('tm')
The draws below stay inside these ranges and needn't reach their ends.
Inputs may be any that keep to these rules, and one draw needn't show every extreme that they name: `shift_steps`: every distance from 1 to 7 is taken by at least one source timeslice. `spin_choice`: each entry is alpha 4 + beta for a pair of spin indices.
All inputs are finite; a program needn't handle non-finite values.
Results may differ from the reference program's by a relative error of at most 0.0003.
Values sent between devices are 32-bit elements; how exact they have to be, the bound alone decides.
No kernel may reach another device: no remote copies, remote signals or barrier semaphores. Data moves between devices by JAX's collectives and lax.ppermute only.
A program may use at most 64 MiB of HBM per device.

```python
import math
import jax
import jax.numpy as jnp
from jax import lax

NVEC = 64
SPIN = 4
COMBOS = 4
NSITES = 8192
NT = 8


def draw_shift_steps(key, part):
    every_step = jnp.arange(1, NT, dtype=jnp.int32)
    extra_step = jax.random.randint(jax.random.fold_in(key, 17), (1,), 1, NT, dtype=jnp.int32)
    pooled = jnp.concatenate([every_step, extra_step], axis=0)
    return jax.random.permutation(jax.random.fold_in(key, 29), pooled).astype(jnp.int32)


def with_ends(entries, stream_key, smallest, top_value):
    index_at = [jax.random.randint(jax.random.fold_in(stream_key, axis), (), 0, length) for axis, length in enumerate(entries.shape)]
    longest = entries.shape.index(max(entries.shape))
    beside = index_at[:longest] + [(index_at[longest] + 1) % entries.shape[longest]] + index_at[longest + 1:]
    return entries.at[tuple(index_at)].set(smallest).at[tuple(beside)].set(top_value)


def shard_levels(own_key, dims, pieces, low, largest):
    factor_of = 1.0
    for axis_at, blocks in pieces:
        heights = jax.random.uniform(jax.random.fold_in(jax.random.fold_in(own_key, 6), axis_at), (blocks,), jnp.float32, low / len(pieces), largest / len(pieces))
        factor_of = factor_of * jnp.repeat(jnp.exp(heights), dims[axis_at] // blocks).reshape((-1,) + (1,) * (len(dims) - 1 - axis_at))
    return factor_of


def gaussian(stream_key, shape, spread, limit, pieces=(), kind=jnp.bfloat16):
    array = spread * jax.random.normal(stream_key, shape, jnp.float32)
    if pieces:
        array = array * shard_levels(stream_key, shape, pieces, -0.22, 0.18)
    return jnp.clip(array, -limit, limit).astype(kind)


def setup_inputs(seed: int = 0) -> dict:
    streams_of = jax.random.split(jax.random.key(seed), 5)
    return {
        "vectors": gaussian(streams_of[0], (NT, 2, 3, NVEC, NSITES), 1.0, 6.0, ((0, 8), (4, 32)), jnp.float32),
        "perambulators": gaussian(streams_of[1], (NT, SPIN * SPIN, 2, NVEC * NVEC), NVEC ** -0.5, 0.75, ((0, 8),), jnp.float32),
        "shift_steps": draw_shift_steps(jax.random.fold_in(streams_of[4], 71), 0),
        "spin_choice": with_ends(jax.random.randint(streams_of[3], (COMBOS, 3), 0, SPIN * SPIN), jax.random.fold_in(streams_of[3], 1), 0, (SPIN * SPIN) - 1).astype(jnp.int32),
    }


exact_mode = lax.Precision.HIGHEST

def complex_product(left_re, left_im, right_re, right_im):
    return (left_re * right_re - left_im * right_im, left_re * right_im + left_im * right_re)

def rotate(values, places):
    return jnp.concatenate([values[places:], values[:places]], axis=0)

def contract_first(left, right):
    return lax.dot_general(left, right, (((0,), (0,)), ((), ())), precision=exact_mode)

def inner_rows(left, right):
    return lax.dot_general(left, right, (((1,), (1,)), ((), ())), precision=exact_mode)

def complex_einsum(form, left, right):
    first = jnp.einsum(form, left[0], right[0], precision=exact_mode) - jnp.einsum(form, left[1], right[1], precision=exact_mode)
    second = jnp.einsum(form, left[0], right[1], precision=exact_mode) + jnp.einsum(form, left[1], right[0], precision=exact_mode)
    return (first, second)

def elemental_rows(vec_re, vec_im, lead_re, lead_im, first_row, row_count, factor):
    sites = vec_re.shape[1]
    nvec = vec_re.shape[2]
    block = math.gcd(row_count, 4)

    def one_block(index):
        offset = (first_row + index * block).astype(jnp.int32)
        part_re = lax.dynamic_slice_in_dim(vec_re, offset, block, 2)[:, :, :, None]
        part_im = lax.dynamic_slice_in_dim(vec_im, offset, block, 2)[:, :, :, None]
        full_re = vec_re[:, :, None, :]
        full_im = vec_im[:, :, None, :]
        one_re, one_im = complex_product(rotate(part_re, 1), rotate(part_im, 1), rotate(full_re, 2), rotate(full_im, 2))
        two_re, two_im = complex_product(rotate(part_re, 2), rotate(part_im, 2), rotate(full_re, 1), rotate(full_im, 1))
        cross_re = (one_re - two_re).reshape(3 * sites, block * nvec)
        cross_im = (one_im - two_im).reshape(3 * sites, block * nvec)
        out_re = contract_first(lead_re, cross_re) - contract_first(lead_im, cross_im)
        out_im = contract_first(lead_re, cross_im) + contract_first(lead_im, cross_re)
        stacked = jnp.stack([out_re, out_im], 0).reshape(2, nvec, block, nvec)
        return jnp.transpose(stacked, (2, 0, 1, 3)).reshape(block, 2, nvec * nvec) * factor
    result = lax.map(one_block, jnp.arange(row_count // block, dtype=jnp.int32))
    return result.reshape(row_count, 2, nvec * nvec)

def transform_rows(own, mats, nvec):
    combos = mats.shape[0]
    row_count = own.shape[0]
    elem = (own[:, 0].reshape(row_count, nvec, nvec), own[:, 1].reshape(row_count, nvec, nvec))
    first_mat = (mats[:, 0, 0].reshape(combos, nvec, nvec), mats[:, 0, 1].reshape(combos, nvec, nvec))
    third_mat = (mats[:, 2, 0].reshape(combos, nvec, nvec), mats[:, 2, 1].reshape(combos, nvec, nvec))
    half = complex_einsum('jik,slk->sjil', elem, third_mat)
    done = complex_einsum('smi,sjil->sjml', first_mat, half)
    return (done[0].reshape(combos * row_count, nvec * nvec), done[1].reshape(combos * row_count, nvec * nvec))

def pair_sum(sink_rows, trans_re, trans_im, mid_re, mid_im):
    combos = mid_re.shape[0]
    sink_count = sink_rows.shape[0]
    own_count = mid_re.shape[2]
    sink_re = sink_rows[:, 0]
    sink_im = sink_rows[:, 1]
    inner_re = (inner_rows(sink_re, trans_re) + inner_rows(sink_im, trans_im)).reshape(sink_count, combos, own_count)
    inner_im = (inner_rows(sink_re, trans_im) - inner_rows(sink_im, trans_re)).reshape(sink_count, combos, own_count)
    total_re = jnp.einsum('srj,rsj->s', mid_re, inner_re, precision=exact_mode) - jnp.einsum('srj,rsj->s', mid_im, inner_im, precision=exact_mode)
    total_im = jnp.einsum('srj,rsj->s', mid_re, inner_im, precision=exact_mode) + jnp.einsum('srj,rsj->s', mid_im, inner_re, precision=exact_mode)
    return jnp.stack([total_re, total_im], -1)

def reference(vectors, perambulators, shift_steps, spin_choice):
    factor = 1.0 / math.sqrt(24.0 * NSITES)
    corr_factor = 0.25 / (NVEC * math.sqrt(NVEC))

    def one_time(vec):
        vec_re = jnp.transpose(vec[0], (0, 2, 1))
        vec_im = jnp.transpose(vec[1], (0, 2, 1))
        lead_re = vec_re.reshape(3 * NSITES, NVEC)
        lead_im = vec_im.reshape(3 * NSITES, NVEC)
        return elemental_rows(vec_re, vec_im, lead_re, lead_im, 0, NVEC, factor)
    elementals = lax.map(one_time, vectors)
    targets = ((jnp.arange(NT, dtype=jnp.int32) + shift_steps.astype(jnp.int32)) % NT).astype(jnp.int32)
    sinks = jnp.take(elementals, targets, axis=0)

    def one_pair(packed):
        own, sink, peram = packed
        mats = peram[spin_choice]
        trans_re, trans_im = transform_rows(own, mats, NVEC)
        mid_re = mats[:, 1, 0].reshape(COMBOS, NVEC, NVEC)
        mid_im = mats[:, 1, 1].reshape(COMBOS, NVEC, NVEC)
        return pair_sum(sink, trans_re, trans_im, mid_re, mid_im) * corr_factor
    correlator = lax.map(one_pair, (elementals, sinks, perambulators))
    return (elementals, correlator)
```

```python
import functools
import math

import jax
import jax.numpy as jnp
from jax import lax
from jax.experimental import pallas as pl
from jax.experimental.pallas import tpu as pltpu
from jax.sharding import Mesh
from jax.sharding import PartitionSpec as P

F32 = jnp.float32
BF16 = jnp.bfloat16
HALF = 32
STEPS = 16
LEAD = (1, 0, 2)


def split(value):
    high = value.astype(BF16)
    return high, (value - high.astype(F32)).astype(BF16)


def dot_nn(left, right):
    return lax.dot_general(left, right, (((1,), (0,)), ((), ())), preferred_element_type=F32)


def dot_nt(left, right):
    return lax.dot_general(left, right, (((1,), (1,)), ((), ())), preferred_element_type=F32)


def dot_tn(left, right):
    return lax.dot_general(left, right, (((0,), (0,)), ((), ())), preferred_element_type=F32)


def lanes_of(shape):
    return lax.broadcasted_iota(jnp.int32, shape, 1)


def pair_kernel(factor, half_ref, vec_ref, out_ref, ext, lead, cross_high, cross_low):
    half = half_ref[0]
    own = pl.multiple_of(half * HALF, HALF)
    other = pl.multiple_of((1 - half) * HALF, HALF)
    for part in range(2):
        for colour in range(3):
            ext[part * 3 + colour, 0:HALF] = vec_ref[part, colour, pl.ds(own, HALF), :]
            ext[part * 3 + colour, HALF : HALF + STEPS] = vec_ref[part, colour, pl.ds(own, STEPS), :]
    sites = vec_ref.shape[3]
    for colour in range(3):
        at = colour * 2 * sites
        own_re, own_im = ext[colour, 0:HALF], ext[3 + colour, 0:HALF]
        oth_re = vec_ref[0, colour, pl.ds(other, HALF), :]
        oth_im = vec_ref[1, colour, pl.ds(other, HALF), :]
        for place, value in enumerate(
            (
                (own_re, -own_im),
                (own_im, own_re),
                (oth_re, -oth_im),
                (oth_im, oth_re),
            )
        ):
            for side in range(2):
                high, low = split(value[side])
                columns = slice(at + side * sites, at + (side + 1) * sites)
                lead[place * HALF : (place + 1) * HALF, columns] = high
                lead[128 + place * HALF : 128 + (place + 1) * HALF, columns] = low
    for group in range(STEPS // 4):
        rows = slice(group * 128, (group + 1) * 128)
        for inner in range(4):
            step = group * 4 + inner + 1
            here = slice(group * 128 + inner * HALF, group * 128 + (inner + 1) * HALF)
            for colour in range(3):
                one, two = (colour + 1) % 3, (colour + 2) % 3
                one_re, one_im = ext[one, 0:HALF], ext[3 + one, 0:HALF]
                two_re, two_im = ext[two, 0:HALF], ext[3 + two, 0:HALF]
                one_re2, one_im2 = ext[one, step : step + HALF], ext[3 + one, step : step + HALF]
                two_re2, two_im2 = ext[two, step : step + HALF], ext[3 + two, step : step + HALF]
                re = (one_re * two_re2 - one_im * two_im2) - (two_re * one_re2 - two_im * one_im2)
                im = (one_re * two_im2 + one_im * two_re2) - (two_re * one_im2 + two_im * one_re2)
                at = colour * 2 * sites
                for side, value in enumerate((re, im)):
                    high, low = split(value)
                    columns = slice(at + side * sites, at + (side + 1) * sites)
                    cross_high[here, columns] = high
                    cross_low[here, columns] = low
        first = dot_nt(cross_high[rows], lead[...])
        second = dot_nt(cross_low[rows], lead[0:128])
        total = (first[:, 0:128] + first[:, 128:256] + second) * (-factor)
        for inner in range(4):
            out_ref[pl.ds(group * 4 + inner, HALF, stride=STEPS), :] = total[inner * HALF : (inner + 1) * HALF]


def pair_products(half, vec, factor):
    sites = vec.shape[3]
    return pl.pallas_call(
        functools.partial(pair_kernel, factor),
        out_shape=jax.ShapeDtypeStruct((HALF * STEPS, 128), F32),
        in_specs=[pl.BlockSpec(memory_space=pltpu.SMEM), pl.BlockSpec(memory_space=pltpu.VMEM)],
        out_specs=pl.BlockSpec(memory_space=pltpu.VMEM),
        scratch_shapes=[
            pltpu.VMEM((6, HALF + STEPS, sites), F32),
            pltpu.VMEM((256, 6 * sites), BF16),
            pltpu.VMEM((HALF * STEPS, 6 * sites), BF16),
            pltpu.VMEM((HALF * STEPS, 6 * sites), BF16),
        ],
        compiler_params=pltpu.CompilerParams(vmem_limit_bytes=24 << 20),
        name="pair_products",
    )(half, vec)


def swap_parts(value):
    lane = lanes_of(value.shape)
    return jnp.where(lane % 64 < 32, pltpu.roll(value, 96, 1), pltpu.roll(value, 32, 1))


def contract_kernel(place_ref, choice_ref, mine_ref, theirs_ref, sink_ref, peram_ref,
                    rows_ref, corr_ref, pairs, quark, weights, inner):
    core, run = place_ref[0], place_ref[1]
    first = core == 0
    combos = choice_ref.shape[0]

    for s in range(combos):
        for q in range(3):
            spin = choice_ref[s, q]
            parts = []
            for part in range(2):
                top = peram_ref[spin, part, pl.ds(pl.multiple_of(core * HALF, HALF), HALF), :]
                low = peram_ref[spin, part, pl.ds(pl.multiple_of((1 - core) * HALF, HALF), HALF), :]
                both = jnp.concatenate([top, low], axis=0)
                left, right = both[:, 0:HALF], both[:, HALF : 2 * HALF]
                parts.append((jnp.where(first, left, right), jnp.where(first, right, left)))
            (re_own, re_oth), (im_own, im_oth) = parts
            quark[s * 3 + q] = jnp.concatenate([re_own, im_own, re_oth, im_oth], axis=1)

    for s in range(combos):
        for slot in range(3):
            for e in range(2):
                row = s * 6 + slot * 2 + e
                weights[row : row + 1] = quark[s * 3 + LEAD[slot], pl.ds(2 * run + e, 1), :]
    tail = 6 * combos
    shape = (HALF - tail, 128)
    lane, row = lanes_of(shape), lax.broadcasted_iota(jnp.int32, shape, 0)
    number = 4 * run + 2 * core + row
    in_own = (number >= HALF) == (core == 1)
    lit = (number % HALF + jnp.where(in_own, 0, 64)) == lane
    weights[tail:HALF] = jnp.where(lit & (row < 2), 1.0, 0.0)

    for g, from_ref in enumerate((mine_ref, theirs_ref)):
        base = g * HALF * HALF
        pairs[pl.ds(base, HALF, stride=HALF + 1), :] = jnp.zeros((HALF, 128), F32)
        for j in range(HALF):
            straight = min(STEPS, HALF - 1 - j)
            at = base + j * HALF
            if straight:
                pairs[at + j + 1 : at + j + 1 + straight] = from_ref[j * STEPS : j * STEPS + straight]
            if straight < STEPS:
                pairs[at : at + STEPS - straight] = from_ref[j * STEPS + straight : (j + 1) * STEPS]
        for j in range(HALF):
            count = STEPS - 1
            straight = min(count, HALF - 1 - j)
            if straight:
                pairs[pl.ds(base + (j + 1) * HALF + j, straight, stride=HALF), :] = -from_ref[j * STEPS : j * STEPS + straight]
            if straight < count:
                pairs[pl.ds(base + j, count - straight, stride=HALF), :] = -from_ref[j * STEPS + straight : j * STEPS + count]

    lead = weights[...]
    wide = lanes_of((HALF, 128))
    sign = jnp.where(wide % 64 < 32, 1.0, -1.0)
    lead_high, lead_low = split(lead)
    conj_high, conj_low = split(lead * sign)
    blank = jnp.zeros((HALF, 64), BF16)
    for g in range(2):
        here = slice(g * 64, g * 64 + 64)
        there = slice(64 - g * 64, 128 - g * 64)
        left_r = jnp.concatenate(
            [
                jnp.concatenate([-lead_high[:, here], -lead_high[:, here]], axis=1),
                jnp.concatenate([-lead_low[:, here], blank], axis=1),
            ],
            axis=0,
        )
        left_n = jnp.concatenate(
            [
                jnp.concatenate([conj_high[:, there], conj_high[:, there]], axis=1),
                jnp.concatenate([conj_low[:, there], blank], axis=1),
            ],
            axis=0,
        )
        for b in range(0, HALF, 2):
            right_r, right_n = [], []
            for e in range(2):
                at = (g * HALF + b + e) * HALF
                value = pairs[at : at + HALF]
                turned = -swap_parts(value) * sign
                parts, packs = [], []
                for one in (value, turned):
                    high = one.astype(BF16)
                    low = one - high.astype(F32)
                    parts.append((high, low.astype(BF16)))
                    packs.append(jnp.where(wide < 64, pltpu.roll(high.astype(F32), 64, 1), low))
                right_r.append(jnp.concatenate([parts[0][0], parts[1][0], parts[0][1], parts[1][1]], axis=0))
                right_n += [packs[0].astype(BF16), (-packs[1]).astype(BF16)]
            some = dot_nn(left_r, jnp.concatenate(right_r, axis=1))
            some = some[0:HALF] + some[HALF : 2 * HALF]
            more = dot_nt(left_n, jnp.concatenate(right_n, axis=0))
            more = more[0:HALF] + more[HALF : 2 * HALF]
            for e in range(2):
                extra = more if e == 0 else pltpu.roll(more, 64, 1)
                result = some[:, e * 128 : (e + 1) * 128] + jnp.where(wide < 64, extra, 0.0)
                if g == 1:
                    result = pltpu.roll(result, 64, 1)
                inner[pl.ds(g * HALF + b + e, HALF, stride=64), :] = result

    for e in range(2):
        at = (tail + e) * 64
        value = inner[at : at + 64]
        shape = (64, 64)
        mixed = (lax.broadcasted_iota(jnp.int32, shape, 0) < HALF) != (lanes_of(shape) < HALF)
        for part in range(2):
            one = jnp.concatenate(
                [value[:, part * 32 : part * 32 + 32], value[:, 64 + part * 32 : 96 + part * 32]], axis=1
            )
            one = one - jnp.where(mixed, one, 0.0).T
            top = jnp.where(first, one[0:HALF], one[HALF:64])
            low = jnp.where(first, one[HALF:64], one[0:HALF])
            both = jnp.concatenate([top, low], axis=0)
            left, right = both[:, 0:HALF], both[:, HALF:64]
            rows_ref[e, part] = jnp.concatenate(
                [jnp.where(first, left, right), jnp.where(first, right, left)], axis=1
            )

    shape = (STEPS, 128)
    step = lax.broadcasted_iota(jnp.int32, shape, 0)
    share = jnp.where(lanes_of(shape) < 64, 1.0 / 3.0, 1.0) * jnp.where(step == STEPS - 1, 0.5, 1.0)
    sink = []
    for e in range(2):
        shape = (HALF, STEPS)
        target = (2 * run + e + lanes_of(shape) + 1) % HALF
        move = jnp.where(lax.broadcasted_iota(jnp.int32, shape, 0) == target, 1.0, 0.0).astype(BF16)
        high, low = split(sink_ref[e * STEPS : (e + 1) * STEPS] * share)
        placed = dot_nn(move, high) + dot_nn(move, low)
        for part in range(2):
            one = jnp.concatenate(
                [placed[:, part * 32 : part * 32 + 32], placed[:, 64 + part * 32 : 96 + part * 32]], axis=1
            )
            one = jnp.concatenate([one, jnp.zeros((HALF, 64), F32)], axis=0)
            sink.append(one - one.T)
    sink_high, sink_low = split(jnp.concatenate(sink, axis=1))
    sink_stack = jnp.concatenate([sink_high, sink_low, sink_high], axis=0)

    shape = (128, 128)
    row, lane = lax.broadcasted_iota(jnp.int32, shape, 0), lanes_of(shape)
    cross = (row % 64 < HALF) != (lane < 64)
    side = jnp.where(lanes_of((64, 128)) < 64, 1.0, -1.0)
    plain = jnp.where(lanes_of((64, 128)) % 64 < 32, 1.0, -1.0)
    results = []
    for s in range(combos):
        dual, both = [], []
        for q in range(3):
            value = quark[s * 3 + q]
            high, low = split(value)
            out = dot_tn(jnp.concatenate([high, high, low], axis=0), sink_stack)
            re = jnp.concatenate([out[0:32], out[64:96]], axis=0)
            im = jnp.concatenate([out[32:64], out[96:128]], axis=0)
            per_row = []
            for e in range(2):
                re_e, im_e = re[:, e * 128 : (e + 1) * 128], im[:, e * 128 : (e + 1) * 128]
                per_row.append(
                    (
                        re_e + pltpu.roll(im_e, 64, 1) * side,
                        im_e - pltpu.roll(re_e, 64, 1) * side,
                    )
                )
            dual.append(per_row)
            full_high, full_low = split(jnp.concatenate([value * plain, swap_parts(value)], axis=0))
            both.append(jnp.concatenate([full_high, full_low], axis=0))
        at = s * 6 * 64
        blocks = [inner[at + slot * 128 : at + (slot + 1) * 128] for slot in range(3)]
        masked = [jnp.where(cross, block, 0.0) for block in blocks]
        acc_re, acc_im = jnp.zeros((64, 128), F32), jnp.zeros((64, 128), F32)
        for q, lefts, partners in (
            (2, (blocks[0], blocks[1]), (0, 1)),
            (1, (blocks[2], masked[1]), (0, 2)),
            (0, (masked[0], masked[2]), (2, 1)),
        ):
            high, low = split(jnp.concatenate(lefts, axis=0))
            out = dot_nt(high, both[q])
            out = out[:, 0:128] + out[:, 128:256] + dot_nt(low, both[q][0:128])
            for k in range(2):
                for e in range(2):
                    part = out[(k * 2 + e) * 64 : (k * 2 + e + 1) * 64]
                    acc_re += part * dual[partners[k]][e][0]
                    acc_im += part * dual[partners[k]][e][1]
        results += [jnp.sum(acc_re, axis=0, keepdims=True), jnp.sum(acc_im, axis=0, keepdims=True)]
    table = jnp.sum(jnp.concatenate(results, axis=0), axis=1, keepdims=True)
    shape = (2 * combos, 128)
    spread = jnp.where(lax.broadcasted_iota(jnp.int32, shape, 0) == lanes_of(shape), table, 0.0)
    corr_ref[...] = jnp.broadcast_to(jnp.sum(spread, axis=0, keepdims=True), corr_ref.shape)


def contract(place, choice, mine, theirs, sink, peram, copies):
    smem = pl.BlockSpec(memory_space=pltpu.SMEM)
    vmem = pl.BlockSpec(memory_space=pltpu.VMEM)
    return pl.pallas_call(
        contract_kernel,
        out_shape=(
            jax.ShapeDtypeStruct((2, 2, 64, 64), F32),
            jax.ShapeDtypeStruct((copies, 128), F32),
        ),
        in_specs=[smem, smem, vmem, vmem, vmem, vmem],
        out_specs=(vmem, vmem),
        scratch_shapes=[
            pltpu.VMEM((2 * HALF * HALF, 128), F32),
            pltpu.VMEM((12, 64, 128), F32),
            pltpu.VMEM((HALF, 128), F32),
            pltpu.VMEM((HALF * 64, 128), F32),
        ],
        compiler_params=pltpu.CompilerParams(vmem_limit_bytes=24 << 20),
        name="contract",
    )(place, choice, mine, theirs, sink, peram)


def swapped(value, axis, mask):
    count = lax.axis_size(axis)
    return lax.ppermute(value, axis, [(i, i ^ mask) for i in range(count)])


def shards(vectors, perambulators, shift_steps, spin_choice):
    vec = vectors[0]
    nvec = vec.shape[2]
    z_count, run_count = lax.axis_size("z"), lax.axis_size("z") * lax.axis_size("yl")
    space_count = run_count * lax.axis_size("core")
    combos = spin_choice.shape[0]
    factor = 1.0 / math.sqrt(24.0 * vec.shape[3] * space_count)
    corr_factor = 0.25 / (nvec * math.sqrt(nvec))
    core = lax.axis_index("core")
    run = lax.axis_index("z") * lax.axis_size("yl") + lax.axis_index("yl")
    peram = perambulators[0].reshape(-1, 2, nvec, nvec)

    away = pair_products((1 - core)[None], vec, factor)
    got = swapped(away, "core", 1)
    keep = pair_products(core[None], vec, factor)
    part = (keep + got).reshape(run_count, -1, 128)
    own = lax.all_to_all(part, ("z", "yl"), 0, 0, tiled=True).sum(0)

    near = jnp.stack([own, swapped(own, "yh", 1)])
    every = jnp.broadcast_to(own[None], (run_count,) + own.shape)
    mine = lax.all_to_all(every, ("z", "yl"), 0, 0, tiled=True).reshape(-1, 128)
    theirs = swapped(mine, "core", 1)
    wider = jnp.concatenate([near, swapped(near, "x", 1)])
    all_times = jnp.concatenate([wider, swapped(wider, "x", 2)])
    now = lax.axis_index("yh") * lax.axis_size("x") + lax.axis_index("x")
    away_by = now ^ ((now + shift_steps[0]) % 8)
    pick = (away_by & 2) * 2 + (away_by & 1) * 2 + (away_by >> 2)
    sink = lax.dynamic_index_in_dim(all_times, pick, 0, keepdims=False)

    place = jnp.stack([core, run]).astype(jnp.int32)
    rows, corr = contract(place, spin_choice, mine, theirs, sink, peram, space_count)
    total = lax.all_to_all(corr, ("z", "yl", "core"), 0, 0, tiled=True).sum(0)
    correlator = total[: 2 * combos].reshape(1, combos, 2) * corr_factor
    return (rows.reshape(1, 2, 2, nvec * nvec)[0], correlator)


def solution(mesh):
    fine = Mesh(mesh.devices.reshape(2, 4, 8, 2, 2), ("yh", "x", "z", "yl", "core"))
    times, space = ("yh", "x"), ("z", "yl", "core")
    placed = (P(times, None, None, None, space), P(times, None, None, None), P(times), P())

    def whole(vectors, perambulators, shift_steps, spin_choice):
        rows, correlator = shards(vectors, perambulators, shift_steps, spin_choice)
        return rows[None], correlator

    return jax.shard_map(
        whole,
        mesh=fine,
        in_specs=placed,
        out_specs=(P(times, space, None, None), P(times, None, None)),
        check_vma=False,
    )
```

```python
import functools
import math

import jax
import jax.numpy as jnp
from jax import lax
from jax.experimental import pallas as pl
from jax.experimental.pallas import tpu as pltpu
from jax.sharding import Mesh
from jax.sharding import PartitionSpec as P

F32 = jnp.float32
BF16 = jnp.bfloat16
HALF = 32
STEPS = 16
LEAD = (1, 0, 2)


def split(value):
    high = value.astype(BF16)
    return high, (value - high.astype(F32)).astype(BF16)


def dot_nn(left, right):
    return lax.dot_general(left, right, (((1,), (0,)), ((), ())), preferred_element_type=F32)


def dot_nt(left, right):
    return lax.dot_general(left, right, (((1,), (1,)), ((), ())), preferred_element_type=F32)


def dot_tn(left, right):
    return lax.dot_general(left, right, (((0,), (0,)), ((), ())), preferred_element_type=F32)


def lanes_of(shape):
    return lax.broadcasted_iota(jnp.int32, shape, 1)


def pair_kernel(factor, half_ref, vec_ref, out_ref, ext, lead, cross_high, cross_low):
    half = half_ref[0]
    own = pl.multiple_of(half * HALF, HALF)
    other = pl.multiple_of((1 - half) * HALF, HALF)
    for part in range(2):
        for colour in range(3):
            ext[part * 3 + colour, 0:HALF] = vec_ref[part, colour, pl.ds(own, HALF), :]
            ext[part * 3 + colour, HALF : HALF + STEPS] = vec_ref[part, colour, pl.ds(own, STEPS), :]
    sites = vec_ref.shape[3]
    for colour in range(3):
        at = colour * 2 * sites
        own_re, own_im = ext[colour, 0:HALF], ext[3 + colour, 0:HALF]
        oth_re = vec_ref[0, colour, pl.ds(other, HALF), :]
        oth_im = vec_ref[1, colour, pl.ds(other, HALF), :]
        for place, value in enumerate(
            (
                (own_re, -own_im),
                (own_im, own_re),
                (oth_re, -oth_im),
                (oth_im, oth_re),
            )
        ):
            for side in range(2):
                high, low = split(value[side])
                columns = slice(at + side * sites, at + (side + 1) * sites)
                lead[place * HALF : (place + 1) * HALF, columns] = high
                lead[128 + place * HALF : 128 + (place + 1) * HALF, columns] = low
    for group in range(STEPS // 4):
        rows = slice(group * 128, (group + 1) * 128)
        for inner in range(4):
            step = group * 4 + inner + 1
            here = slice(group * 128 + inner * HALF, group * 128 + (inner + 1) * HALF)
            for colour in range(3):
                one, two = (colour + 1) % 3, (colour + 2) % 3
                one_re, one_im = ext[one, 0:HALF], ext[3 + one, 0:HALF]
                two_re, two_im = ext[two, 0:HALF], ext[3 + two, 0:HALF]
                one_re2, one_im2 = ext[one, step : step + HALF], ext[3 + one, step : step + HALF]
                two_re2, two_im2 = ext[two, step : step + HALF], ext[3 + two, step : step + HALF]
                re = (one_re * two_re2 - one_im * two_im2) - (two_re * one_re2 - two_im * one_im2)
                im = (one_re * two_im2 + one_im * two_re2) - (two_re * one_im2 + two_im * one_re2)
                at = colour * 2 * sites
                for side, value in enumerate((re, im)):
                    high, low = split(value)
                    columns = slice(at + side * sites, at + (side + 1) * sites)
                    cross_high[here, columns] = high
                    cross_low[here, columns] = low
        first = dot_nt(cross_high[rows], lead[...])
        second = dot_nt(cross_low[rows], lead[0:128])
        total = (first[:, 0:128] + first[:, 128:256] + second) * (-factor)
        for inner in range(4):
            out_ref[pl.ds(group * 4 + inner, HALF, stride=STEPS), :] = total[inner * HALF : (inner + 1) * HALF]


def pair_products(half, vec, factor):
    sites = vec.shape[3]
    return pl.pallas_call(
        functools.partial(pair_kernel, factor),
        out_shape=jax.ShapeDtypeStruct((HALF * STEPS, 128), F32),
        in_specs=[pl.BlockSpec(memory_space=pltpu.SMEM), pl.BlockSpec(memory_space=pltpu.VMEM)],
        out_specs=pl.BlockSpec(memory_space=pltpu.VMEM),
        scratch_shapes=[
            pltpu.VMEM((6, HALF + STEPS, sites), F32),
            pltpu.VMEM((256, 6 * sites), BF16),
            pltpu.VMEM((HALF * STEPS, 6 * sites), BF16),
            pltpu.VMEM((HALF * STEPS, 6 * sites), BF16),
        ],
        compiler_params=pltpu.CompilerParams(vmem_limit_bytes=24 << 20),
        name="pair_products",
    )(half, vec)


def swap_parts(value):
    lane = lanes_of(value.shape)
    return jnp.where(lane % 64 < 32, pltpu.roll(value, 96, 1), pltpu.roll(value, 32, 1))


def turned(value, sign):
    return -swap_parts(value) * sign


def part_signs(shape):
    return jnp.where(lanes_of(shape) % 64 < 32, 1.0, -1.0)


def prepare_kernel(place_ref, choice_ref, peram_ref, left_r_ref, left_n_ref, flipped_ref, full_ref, quark, weights):
    core, run = place_ref[0], place_ref[1]
    first = core == 0
    combos = choice_ref.shape[0]
    plain = part_signs((64, 128))
    for s in range(combos):
        for q in range(3):
            spin = choice_ref[s, q]
            parts = []
            for part in range(2):
                top = peram_ref[spin, part, pl.ds(pl.multiple_of(core * HALF, HALF), HALF), :]
                low = peram_ref[spin, part, pl.ds(pl.multiple_of((1 - core) * HALF, HALF), HALF), :]
                both = jnp.concatenate([top, low], axis=0)
                left, right = both[:, 0:HALF], both[:, HALF : 2 * HALF]
                parts.append((jnp.where(first, left, right), jnp.where(first, right, left)))
            (re_own, re_oth), (im_own, im_oth) = parts
            value = jnp.concatenate([re_own, im_own, re_oth, im_oth], axis=1)
            quark[s * 3 + q] = value
            high, low = split(value.T)
            flipped_ref[s * 3 + q] = jnp.concatenate([high, high, low], axis=1)
            full_high, full_low = split(jnp.concatenate([value * plain, swap_parts(value)], axis=0))
            full_ref[s * 3 + q] = jnp.concatenate([full_high, full_low], axis=0)

    for s in range(combos):
        for slot in range(3):
            for e in range(2):
                row = s * 6 + slot * 2 + e
                weights[row : row + 1] = quark[s * 3 + LEAD[slot], pl.ds(2 * run + e, 1), :]
    tail = 6 * combos
    shape = (HALF - tail, 128)
    lane, row = lanes_of(shape), lax.broadcasted_iota(jnp.int32, shape, 0)
    number = 4 * run + 2 * core + row
    in_own = (number >= HALF) == (core == 1)
    lit = (number % HALF + jnp.where(in_own, 0, 64)) == lane
    weights[tail:HALF] = jnp.where(lit & (row < 2), 1.0, 0.0)

    lead = weights[...]
    sign = part_signs((HALF, 128))
    lead_high, lead_low = split(lead)
    conj_high, conj_low = split(lead * sign)
    blank = jnp.zeros((HALF, 64), BF16)
    for g in range(2):
        here = slice(g * 64, g * 64 + 64)
        there = slice(64 - g * 64, 128 - g * 64)
        left_r_ref[g, 0:HALF] = jnp.concatenate([-lead_high[:, here], -lead_high[:, here]], axis=1)
        left_r_ref[g, HALF : 2 * HALF] = jnp.concatenate([-lead_low[:, here], blank], axis=1)
        left_n_ref[g, 0:HALF] = jnp.concatenate([conj_high[:, there], conj_high[:, there]], axis=1)
        left_n_ref[g, HALF : 2 * HALF] = jnp.concatenate([conj_low[:, there], blank], axis=1)


def first_index_kernel(left_r_ref, left_n_ref, mine_ref, theirs_ref, inner, pairs):
    for g, from_ref in enumerate((mine_ref, theirs_ref)):
        base = g * HALF * HALF
        pairs[pl.ds(base, HALF, stride=HALF + 1), :] = jnp.zeros((HALF, 128), F32)
        for j in range(HALF):
            straight = min(STEPS, HALF - 1 - j)
            at = base + j * HALF
            if straight:
                pairs[at + j + 1 : at + j + 1 + straight] = from_ref[j * STEPS : j * STEPS + straight]
            if straight < STEPS:
                pairs[at : at + STEPS - straight] = from_ref[j * STEPS + straight : (j + 1) * STEPS]
        for j in range(HALF):
            count = STEPS - 1
            straight = min(count, HALF - 1 - j)
            if straight:
                pairs[pl.ds(base + (j + 1) * HALF + j, straight, stride=HALF), :] = -from_ref[j * STEPS : j * STEPS + straight]
            if straight < count:
                pairs[pl.ds(base + j, count - straight, stride=HALF), :] = -from_ref[j * STEPS + straight : j * STEPS + count]

    wide = lanes_of((HALF, 128))
    sign = part_signs((HALF, 128))
    for g in range(2):
        left_r, left_n = left_r_ref[g], left_n_ref[g]
        for b in range(0, HALF, 2):
            right_r, right_n = [], []
            for e in range(2):
                at = (g * HALF + b + e) * HALF
                value = pairs[at : at + HALF]
                parts, packs = [], []
                for one in (value, turned(value, sign)):
                    high = one.astype(BF16)
                    low = one - high.astype(F32)
                    parts.append((high, low.astype(BF16)))
                    packs.append(jnp.where(wide < 64, pltpu.roll(high.astype(F32), 64, 1), low))
                right_r.append(jnp.concatenate([parts[0][0], parts[1][0], parts[0][1], parts[1][1]], axis=0))
                right_n += [packs[0].astype(BF16), (-packs[1]).astype(BF16)]
            some = dot_nn(left_r, jnp.concatenate(right_r, axis=1))
            some = some[0:HALF] + some[HALF : 2 * HALF]
            more = dot_nt(left_n, jnp.concatenate(right_n, axis=0))
            more = more[0:HALF] + more[HALF : 2 * HALF]
            for e in range(2):
                extra = more if e == 0 else pltpu.roll(more, 64, 1)
                result = some[:, e * 128 : (e + 1) * 128] + jnp.where(wide < 64, extra, 0.0)
                if g == 1:
                    result = pltpu.roll(result, 64, 1)
                inner[pl.ds(g * HALF + b + e, HALF, stride=64), :] = result


def rows_kernel(place_ref, inner_ref, rows_ref):
    first = place_ref[0] == 0
    tail = HALF - 8
    for e in range(2):
        value = inner_ref[(tail + e) * 64 : (tail + e + 1) * 64]
        shape = (64, 64)
        mixed = (lax.broadcasted_iota(jnp.int32, shape, 0) < HALF) != (lanes_of(shape) < HALF)
        for part in range(2):
            one = jnp.concatenate(
                [value[:, part * 32 : part * 32 + 32], value[:, 64 + part * 32 : 96 + part * 32]], axis=1
            )
            one = one - jnp.where(mixed, one, 0.0).T
            top = jnp.where(first, one[0:HALF], one[HALF:64])
            low = jnp.where(first, one[HALF:64], one[0:HALF])
            both = jnp.concatenate([top, low], axis=0)
            left, right = both[:, 0:HALF], both[:, HALF:64]
            rows_ref[e, part] = jnp.concatenate(
                [jnp.where(first, left, right), jnp.where(first, right, left)], axis=1
            )


def correlate_kernel(place_ref, sink_ref, flipped_ref, full_ref, inner_ref, corr_ref):
    run = place_ref[1]
    combos = flipped_ref.shape[0] // 3
    shape = (STEPS, 128)
    step = lax.broadcasted_iota(jnp.int32, shape, 0)
    share = jnp.where(lanes_of(shape) < 64, 1.0 / 3.0, 1.0) * jnp.where(step == STEPS - 1, 0.5, 1.0)
    sink = []
    for e in range(2):
        shape = (HALF, STEPS)
        target = (2 * run + e + lanes_of(shape) + 1) % HALF
        move = jnp.where(lax.broadcasted_iota(jnp.int32, shape, 0) == target, 1.0, 0.0).astype(BF16)
        high, low = split(sink_ref[e * STEPS : (e + 1) * STEPS] * share)
        placed = dot_nn(move, high) + dot_nn(move, low)
        for part in range(2):
            one = jnp.concatenate(
                [placed[:, part * 32 : part * 32 + 32], placed[:, 64 + part * 32 : 96 + part * 32]], axis=1
            )
            one = jnp.concatenate([one, jnp.zeros((HALF, 64), F32)], axis=0)
            sink.append(one - one.T)
    sink_high, sink_low = split(jnp.concatenate(sink, axis=1))
    sink_stack = jnp.concatenate([sink_high, sink_low, sink_high], axis=0)

    shape = (128, 128)
    row, lane = lax.broadcasted_iota(jnp.int32, shape, 0), lanes_of(shape)
    cross = (row % 64 < HALF) != (lane < 64)
    side = jnp.where(lanes_of((64, 128)) < 64, 1.0, -1.0)
    results = []
    for s in range(combos):
        dual = []
        for q in range(3):
            out = dot_nn(flipped_ref[s * 3 + q], sink_stack)
            re = jnp.concatenate([out[0:32], out[64:96]], axis=0)
            im = jnp.concatenate([out[32:64], out[96:128]], axis=0)
            per_row = []
            for e in range(2):
                re_e, im_e = re[:, e * 128 : (e + 1) * 128], im[:, e * 128 : (e + 1) * 128]
                per_row.append(
                    (
                        re_e + pltpu.roll(im_e, 64, 1) * side,
                        im_e - pltpu.roll(re_e, 64, 1) * side,
                    )
                )
            dual.append(per_row)
        at = s * 6 * 64
        blocks = [inner_ref[at + slot * 128 : at + (slot + 1) * 128] for slot in range(3)]
        masked = [jnp.where(cross, block, 0.0) for block in blocks]
        acc_re, acc_im = jnp.zeros((64, 128), F32), jnp.zeros((64, 128), F32)
        for q, lefts, partners in (
            (2, (blocks[0], blocks[1]), (0, 1)),
            (1, (blocks[2], masked[1]), (0, 2)),
            (0, (masked[0], masked[2]), (2, 1)),
        ):
            high, low = split(jnp.concatenate(lefts, axis=0))
            out = dot_nt(high, full_ref[s * 3 + q])
            out = out[:, 0:128] + out[:, 128:256] + dot_nt(low, full_ref[s * 3 + q, 0:128])
            for k in range(2):
                for e in range(2):
                    part = out[(k * 2 + e) * 64 : (k * 2 + e + 1) * 64]
                    acc_re += part * dual[partners[k]][e][0]
                    acc_im += part * dual[partners[k]][e][1]
        results += [jnp.sum(acc_re, axis=0, keepdims=True), jnp.sum(acc_im, axis=0, keepdims=True)]
    table = jnp.sum(jnp.concatenate(results, axis=0), axis=1, keepdims=True)
    shape = (2 * combos, 128)
    spread = jnp.where(lax.broadcasted_iota(jnp.int32, shape, 0) == lanes_of(shape), table, 0.0)
    corr_ref[...] = jnp.broadcast_to(jnp.sum(spread, axis=0, keepdims=True), corr_ref.shape)


SMEM = pl.BlockSpec(memory_space=pltpu.SMEM)
VMEM = pl.BlockSpec(memory_space=pltpu.VMEM)


def call(kernel, name, outs, ins, scratch, micros, args):
    return pl.pallas_call(
        kernel,
        out_shape=outs,
        in_specs=ins,
        out_specs=jax.tree.map(lambda _: VMEM, outs),
        scratch_shapes=scratch,
        compiler_params=pltpu.CompilerParams(vmem_limit_bytes=16 << 20),
        cost_estimate=pl.CostEstimate(flops=0, bytes_accessed=int(micros * 3.5e6), transcendentals=0),
        name=name,
    )(*args)


def shape_of(dtype, *dims):
    return jax.ShapeDtypeStruct(dims, dtype)


def prepare(place, choice, peram):
    count = 3 * choice.shape[0]
    return call(
        prepare_kernel,
        "prepare",
        (
            shape_of(BF16, 2, 64, 128),
            shape_of(BF16, 2, 64, 128),
            shape_of(BF16, count, 128, 192),
            shape_of(BF16, count, 256, 128),
        ),
        [SMEM, SMEM, VMEM],
        [pltpu.VMEM((count, 64, 128), F32), pltpu.VMEM((HALF, 128), F32)],
        3,
        (place, choice, peram),
    )


def first_index(left_r, left_n, mine, theirs):
    return call(
        first_index_kernel,
        "first_index",
        shape_of(F32, HALF * 64, 128),
        [VMEM] * 4,
        [pltpu.VMEM((2 * HALF * HALF, 128), F32)],
        8,
        (left_r, left_n, mine, theirs),
    )


def own_rows(place, inner):
    return call(rows_kernel, "own_rows", shape_of(F32, 2, 2, 64, 64), [SMEM, VMEM], [], 3, (place, inner))


def correlate(place, sink, flipped, full, inner, copies):
    return call(
        correlate_kernel,
        "correlate",
        shape_of(F32, copies, 128),
        [SMEM, VMEM, VMEM, VMEM, VMEM],
        [],
        4,
        (place, sink, flipped, full, inner),
    )


def swapped(value, axis, mask):
    count = lax.axis_size(axis)
    return lax.ppermute(value, axis, [(i, i ^ mask) for i in range(count)])


def shards(vectors, perambulators, shift_steps, spin_choice):
    vec = vectors[0]
    nvec = vec.shape[2]
    z_count, run_count = lax.axis_size("z"), lax.axis_size("z") * lax.axis_size("yl")
    space_count = run_count * lax.axis_size("core")
    combos = spin_choice.shape[0]
    factor = 1.0 / math.sqrt(24.0 * vec.shape[3] * space_count)
    corr_factor = 0.25 / (nvec * math.sqrt(nvec))
    core = lax.axis_index("core")
    run = lax.axis_index("z") * lax.axis_size("yl") + lax.axis_index("yl")
    peram = perambulators[0].reshape(-1, 2, nvec, nvec)

    away = pair_products((1 - core)[None], vec, factor)
    got = swapped(away, "core", 1)
    keep = pair_products(core[None], vec, factor)
    part = (keep + got).reshape(run_count, -1, 128)
    own = lax.all_to_all(part, ("z", "yl"), 0, 0, tiled=True).sum(0)

    place = jnp.stack([core, run]).astype(jnp.int32)
    place, own = lax.optimization_barrier((place, own))
    near = jnp.stack([own, swapped(own, "yh", 1)])
    every = jnp.broadcast_to(own[None], (run_count,) + own.shape)
    mine = lax.all_to_all(every, ("z", "yl"), 0, 0, tiled=True).reshape(-1, 128)
    left_r, left_n, flipped, full = prepare(place, spin_choice, peram)
    theirs = swapped(mine, "core", 1)
    wider = jnp.concatenate([near, swapped(near, "x", 1)])
    all_times = jnp.concatenate([wider, swapped(wider, "x", 2)])
    now = lax.axis_index("yh") * lax.axis_size("x") + lax.axis_index("x")
    away_by = now ^ ((now + shift_steps[0]) % 8)
    pick = (away_by & 2) * 2 + (away_by & 1) * 2 + (away_by >> 2)
    sink = lax.dynamic_index_in_dim(all_times, pick, 0, keepdims=False)

    inner = first_index(left_r, left_n, mine, theirs)
    corr = correlate(place, sink, flipped, full, inner, space_count)
    total = lax.all_to_all(corr, ("z", "yl", "core"), 0, 0, tiled=True).sum(0)
    rows = own_rows(place, inner)
    correlator = total[: 2 * combos].reshape(1, combos, 2) * corr_factor
    return (rows.reshape(1, 2, 2, nvec * nvec)[0], correlator)


def solution(mesh):
    fine = Mesh(mesh.devices.reshape(2, 4, 8, 2, 2), ("yh", "x", "z", "yl", "core"))
    times, space = ("yh", "x"), ("z", "yl", "core")
    placed = (P(times, None, None, None, space), P(times, None, None, None), P(times), P())

    def whole(vectors, perambulators, shift_steps, spin_choice):
        rows, correlator = shards(vectors, perambulators, shift_steps, spin_choice)
        return rows[None], correlator

    return jax.shard_map(
        whole,
        mesh=fine,
        in_specs=placed,
        out_specs=(P(times, space, None, None), P(times, None, None)),
        check_vma=False,
    )
```

```python
import functools
import math

import jax
import jax.numpy as jnp
from jax import lax
from jax.experimental import pallas as pl
from jax.experimental.pallas import tpu as pltpu
from jax.sharding import Mesh
from jax.sharding import PartitionSpec as P

F32 = jnp.float32
BF16 = jnp.bfloat16
HALF = 32
STEPS = 16
LEAD = (1, 0, 2)


def split(value):
    high = value.astype(BF16)
    return high, (value - high.astype(F32)).astype(BF16)


def dot_nn(left, right):
    return lax.dot_general(left, right, (((1,), (0,)), ((), ())), preferred_element_type=F32)


def dot_nt(left, right):
    return lax.dot_general(left, right, (((1,), (1,)), ((), ())), preferred_element_type=F32)


def dot_tn(left, right):
    return lax.dot_general(left, right, (((0,), (0,)), ((), ())), preferred_element_type=F32)


def lanes_of(shape):
    return lax.broadcasted_iota(jnp.int32, shape, 1)


def pair_kernel(factor, half_ref, vec_ref, out_ref, ext, lead, cross_high, cross_low):
    half = half_ref[0]
    own = pl.multiple_of(half * HALF, HALF)
    other = pl.multiple_of((1 - half) * HALF, HALF)
    for part in range(2):
        for colour in range(3):
            ext[part * 3 + colour, 0:HALF] = vec_ref[part, colour, pl.ds(own, HALF), :]
            ext[part * 3 + colour, HALF : HALF + STEPS] = vec_ref[part, colour, pl.ds(own, STEPS), :]
    sites = vec_ref.shape[3]
    for colour in range(3):
        at = colour * 2 * sites
        own_re, own_im = ext[colour, 0:HALF], ext[3 + colour, 0:HALF]
        oth_re = vec_ref[0, colour, pl.ds(other, HALF), :]
        oth_im = vec_ref[1, colour, pl.ds(other, HALF), :]
        for place, value in enumerate(
            (
                (own_re, -own_im),
                (own_im, own_re),
                (oth_re, -oth_im),
                (oth_im, oth_re),
            )
        ):
            for side in range(2):
                high, low = split(value[side])
                columns = slice(at + side * sites, at + (side + 1) * sites)
                lead[place * HALF : (place + 1) * HALF, columns] = high
                lead[128 + place * HALF : 128 + (place + 1) * HALF, columns] = low
    for group in range(STEPS // 4):
        rows = slice(group * 128, (group + 1) * 128)
        for inner in range(4):
            step = group * 4 + inner + 1
            here = slice(group * 128 + inner * HALF, group * 128 + (inner + 1) * HALF)
            for colour in range(3):
                one, two = (colour + 1) % 3, (colour + 2) % 3
                one_re, one_im = ext[one, 0:HALF], ext[3 + one, 0:HALF]
                two_re, two_im = ext[two, 0:HALF], ext[3 + two, 0:HALF]
                one_re2, one_im2 = ext[one, step : step + HALF], ext[3 + one, step : step + HALF]
                two_re2, two_im2 = ext[two, step : step + HALF], ext[3 + two, step : step + HALF]
                re = (one_re * two_re2 - one_im * two_im2) - (two_re * one_re2 - two_im * one_im2)
                im = (one_re * two_im2 + one_im * two_re2) - (two_re * one_im2 + two_im * one_re2)
                at = colour * 2 * sites
                for side, value in enumerate((re, im)):
                    high, low = split(value)
                    columns = slice(at + side * sites, at + (side + 1) * sites)
                    cross_high[here, columns] = high
                    cross_low[here, columns] = low
        first = dot_nt(cross_high[rows], lead[...])
        second = dot_nt(cross_low[rows], lead[0:128])
        total = (first[:, 0:128] + first[:, 128:256] + second) * (-factor)
        for inner in range(4):
            out_ref[pl.ds(group * 4 + inner, HALF, stride=STEPS), :] = total[inner * HALF : (inner + 1) * HALF]


def pair_products(half, vec, factor):
    sites = vec.shape[3]
    return pl.pallas_call(
        functools.partial(pair_kernel, factor),
        out_shape=jax.ShapeDtypeStruct((HALF * STEPS, 128), F32),
        in_specs=[pl.BlockSpec(memory_space=pltpu.SMEM), pl.BlockSpec(memory_space=pltpu.VMEM)],
        out_specs=pl.BlockSpec(memory_space=pltpu.VMEM),
        scratch_shapes=[
            pltpu.VMEM((6, HALF + STEPS, sites), F32),
            pltpu.VMEM((256, 6 * sites), BF16),
            pltpu.VMEM((HALF * STEPS, 6 * sites), BF16),
            pltpu.VMEM((HALF * STEPS, 6 * sites), BF16),
        ],
        compiler_params=pltpu.CompilerParams(vmem_limit_bytes=24 << 20),
        name="pair_products",
    )(half, vec)


def swap_parts(value):
    lane = lanes_of(value.shape)
    return jnp.where(lane % 64 < 32, pltpu.roll(value, 96, 1), pltpu.roll(value, 32, 1))


def turned(value, sign):
    return -swap_parts(value) * sign


def part_signs(shape):
    return jnp.where(lanes_of(shape) % 64 < 32, 1.0, -1.0)


def prepare_kernel(place_ref, choice_ref, peram_ref, left_r_ref, left_n_ref, flipped_ref, full_ref, quark, weights):
    core, run = place_ref[0], place_ref[1]
    first = core == 0
    combos = choice_ref.shape[0]
    plain = part_signs((64, 128))
    for s in range(combos):
        for q in range(3):
            spin = choice_ref[s, q]
            parts = []
            for part in range(2):
                top = peram_ref[spin, part, pl.ds(pl.multiple_of(core * HALF, HALF), HALF), :]
                low = peram_ref[spin, part, pl.ds(pl.multiple_of((1 - core) * HALF, HALF), HALF), :]
                both = jnp.concatenate([top, low], axis=0)
                left, right = both[:, 0:HALF], both[:, HALF : 2 * HALF]
                parts.append((jnp.where(first, left, right), jnp.where(first, right, left)))
            (re_own, re_oth), (im_own, im_oth) = parts
            value = jnp.concatenate([re_own, im_own, re_oth, im_oth], axis=1)
            quark[s * 3 + q] = value
            high, low = split(value.T)
            flipped_ref[s * 3 + q] = jnp.concatenate([high, high, low], axis=1)
            full_high, full_low = split(jnp.concatenate([value * plain, swap_parts(value)], axis=0))
            full_ref[s * 3 + q] = jnp.concatenate([full_high, full_low], axis=0)

    for s in range(combos):
        for slot in range(3):
            for e in range(2):
                row = s * 6 + slot * 2 + e
                weights[row : row + 1] = quark[s * 3 + LEAD[slot], pl.ds(2 * run + e, 1), :]
    tail = 6 * combos
    shape = (HALF - tail, 128)
    lane, row = lanes_of(shape), lax.broadcasted_iota(jnp.int32, shape, 0)
    number = 4 * run + 2 * core + row
    in_own = (number >= HALF) == (core == 1)
    lit = (number % HALF + jnp.where(in_own, 0, 64)) == lane
    weights[tail:HALF] = jnp.where(lit & (row < 2), 1.0, 0.0)

    lead = weights[...]
    sign = part_signs((HALF, 128))
    lead_high, lead_low = split(lead)
    conj_high, conj_low = split(lead * sign)
    cross_high, cross_low = split(swap_parts(lead))
    blank = jnp.zeros((HALF, 64), BF16)
    for g in range(2):
        re, im = slice(g * 64, g * 64 + 32), slice(g * 64 + 32, g * 64 + 64)
        there = slice(64 - g * 64, 128 - g * 64)
        none = jnp.zeros((HALF, 32), BF16)
        for k, rows in enumerate(
            (
                (-lead_high[:, re], -lead_high[:, re]),
                (-lead_high[:, im], -lead_high[:, im]),
                (-lead_low[:, re], none),
                (-lead_low[:, im], none),
            )
        ):
            left_r_ref[g, k * HALF : (k + 1) * HALF] = jnp.concatenate(rows, axis=1)
        for k, (rows, low_rows) in enumerate(
            (
                (conj_high[:, there], conj_high[:, there]),
                (cross_high[:, there], cross_high[:, there]),
                (conj_low[:, there], blank),
                (cross_low[:, there], blank),
            )
        ):
            left_n_ref[g, k * HALF : (k + 1) * HALF] = jnp.concatenate([rows, low_rows], axis=1)


def first_index_kernel(left_r_ref, left_n_ref, mine_ref, theirs_ref, inner, pairs, turned_ref):
    for g in range(2):
        base = g * HALF * HALF
        if g == 0:
            from_ref = mine_ref
        else:
            turned_ref[...] = pltpu.roll(theirs_ref[...], 64, 1)
            from_ref = turned_ref
        pairs[pl.ds(base, HALF, stride=HALF + 1), :] = jnp.zeros((HALF, 128), F32)
        for j in range(HALF):
            straight = min(STEPS, HALF - 1 - j)
            at = base + j * HALF
            if straight:
                pairs[at + j + 1 : at + j + 1 + straight] = from_ref[j * STEPS : j * STEPS + straight]
            if straight < STEPS:
                pairs[at : at + STEPS - straight] = from_ref[j * STEPS + straight : (j + 1) * STEPS]
        for j in range(HALF):
            count = STEPS - 1
            straight = min(count, HALF - 1 - j)
            if straight:
                pairs[pl.ds(base + (j + 1) * HALF + j, straight, stride=HALF), :] = -from_ref[j * STEPS : j * STEPS + straight]
            if straight < count:
                pairs[pl.ds(base + j, count - straight, stride=HALF), :] = -from_ref[j * STEPS + straight : j * STEPS + count]

    wide = lanes_of((HALF, 128))
    sign = part_signs((HALF, 128))
    for g in range(2):
        left_r, left_n = left_r_ref[g], left_n_ref[g]
        here = g * 64
        for b in range(0, HALF, 4):
            stacks, packs = [], []
            for e in range(4):
                at = (g * HALF + b + e) * HALF
                value = pairs[at : at + HALF]
                high = value.astype(BF16)
                full = high.astype(F32)
                low = value - full
                stacks.append(jnp.concatenate([high, low.astype(BF16)], axis=0))
                if g == 0:
                    full = pltpu.roll(full, 64, 1)
                else:
                    low = pltpu.roll(low, 64, 1)
                packs.append(jnp.where(wide < 64, full, low).astype(BF16))
            more = dot_nt(left_n, jnp.concatenate(packs, axis=0))
            more_re = more[0:HALF] + more[2 * HALF : 3 * HALF]
            more_im = more[HALF : 2 * HALF] + more[3 * HALF : 4 * HALF]
            for pair in range(2):
                some = dot_nn(left_r, jnp.concatenate(stacks[2 * pair : 2 * pair + 2], axis=1))
                some_re = some[0:HALF] + some[2 * HALF : 3 * HALF]
                some_im = some[HALF : 2 * HALF] + some[3 * HALF : 4 * HALF]
                for e in range(2):
                    at = (2 * pair + e) * 32
                    columns = slice(e * 128, e * 128 + 128)
                    result = some_re[:, columns] + turned(some_im[:, columns], sign)
                    extra_re, extra_im = more_re, more_im
                    if (here - at) % 128:
                        extra_re = pltpu.roll(extra_re, (here - at) % 128, 1)
                    if (here + 32 - at) % 128:
                        extra_im = pltpu.roll(extra_im, (here + 32 - at) % 128, 1)
                    extra = jnp.where(wide % 64 < 32, extra_re, extra_im)
                    result += jnp.where((wide < 64) == (g == 0), extra, 0.0)
                    inner[pl.ds(g * HALF + b + 2 * pair + e, HALF, stride=64), :] = result


def rows_kernel(place_ref, inner_ref, rows_ref):
    first = place_ref[0] == 0
    tail = HALF - 8
    for e in range(2):
        value = inner_ref[(tail + e) * 64 : (tail + e + 1) * 64]
        shape = (64, 64)
        mixed = (lax.broadcasted_iota(jnp.int32, shape, 0) < HALF) != (lanes_of(shape) < HALF)
        for part in range(2):
            one = jnp.concatenate(
                [value[:, part * 32 : part * 32 + 32], value[:, 64 + part * 32 : 96 + part * 32]], axis=1
            )
            one = one - jnp.where(mixed, one, 0.0).T
            top = jnp.where(first, one[0:HALF], one[HALF:64])
            low = jnp.where(first, one[HALF:64], one[0:HALF])
            both = jnp.concatenate([top, low], axis=0)
            left, right = both[:, 0:HALF], both[:, HALF:64]
            rows_ref[e, part] = jnp.concatenate(
                [jnp.where(first, left, right), jnp.where(first, right, left)], axis=1
            )


def correlate_kernel(place_ref, sink_ref, flipped_ref, full_ref, inner_ref, corr_ref):
    run = place_ref[1]
    combos = flipped_ref.shape[0] // 3
    shape = (STEPS, 128)
    step = lax.broadcasted_iota(jnp.int32, shape, 0)
    share = jnp.where(lanes_of(shape) < 64, 1.0 / 3.0, 1.0) * jnp.where(step == STEPS - 1, 0.5, 1.0)
    sink = []
    for e in range(2):
        shape = (HALF, STEPS)
        target = (2 * run + e + lanes_of(shape) + 1) % HALF
        move = jnp.where(lax.broadcasted_iota(jnp.int32, shape, 0) == target, 1.0, 0.0).astype(BF16)
        high, low = split(sink_ref[e * STEPS : (e + 1) * STEPS] * share)
        placed = dot_nn(move, high) + dot_nn(move, low)
        for part in range(2):
            one = jnp.concatenate(
                [placed[:, part * 32 : part * 32 + 32], placed[:, 64 + part * 32 : 96 + part * 32]], axis=1
            )
            one = jnp.concatenate([one, jnp.zeros((HALF, 64), F32)], axis=0)
            sink.append(one - one.T)
    sink_high, sink_low = split(jnp.concatenate(sink, axis=1))
    sink_stack = jnp.concatenate([sink_high, sink_low, sink_high], axis=0)

    shape = (128, 128)
    row, lane = lax.broadcasted_iota(jnp.int32, shape, 0), lanes_of(shape)
    cross = (row % 64 < HALF) != (lane < 64)
    side = jnp.where(lanes_of((64, 128)) < 64, 1.0, -1.0)
    results = []
    for s in range(combos):
        dual = []
        for q in range(3):
            out = dot_nn(flipped_ref[s * 3 + q], sink_stack)
            re = jnp.concatenate([out[0:32], out[64:96]], axis=0)
            im = jnp.concatenate([out[32:64], out[96:128]], axis=0)
            per_row = []
            for e in range(2):
                re_e, im_e = re[:, e * 128 : (e + 1) * 128], im[:, e * 128 : (e + 1) * 128]
                per_row.append(
                    (
                        re_e + pltpu.roll(im_e, 64, 1) * side,
                        im_e - pltpu.roll(re_e, 64, 1) * side,
                    )
                )
            dual.append(per_row)
        at = s * 6 * 64
        blocks = [inner_ref[at + slot * 128 : at + (slot + 1) * 128] for slot in range(3)]
        masked = [jnp.where(cross, block, 0.0) for block in blocks]
        acc_re, acc_im = jnp.zeros((64, 128), F32), jnp.zeros((64, 128), F32)
        for q, lefts, partners in (
            (2, (blocks[0], blocks[1]), (0, 1)),
            (1, (blocks[2], masked[1]), (0, 2)),
            (0, (masked[0], masked[2]), (2, 1)),
        ):
            high, low = split(jnp.concatenate(lefts, axis=0))
            out = dot_nt(high, full_ref[s * 3 + q])
            out = out[:, 0:128] + out[:, 128:256] + dot_nt(low, full_ref[s * 3 + q, 0:128])
            for k in range(2):
                for e in range(2):
                    part = out[(k * 2 + e) * 64 : (k * 2 + e + 1) * 64]
                    acc_re += part * dual[partners[k]][e][0]
                    acc_im += part * dual[partners[k]][e][1]
        results.append((jnp.sum(acc_re, axis=0, keepdims=True), jnp.sum(acc_im, axis=0, keepdims=True)))
    table = jnp.concatenate([result[part] for part in range(2) for result in results], axis=0)
    table = jnp.sum(table, axis=1, keepdims=True)
    shape = (2 * combos, 128)
    spread = jnp.where(lax.broadcasted_iota(jnp.int32, shape, 0) == lanes_of(shape), table, 0.0)
    corr_ref[...] = jnp.broadcast_to(jnp.sum(spread, axis=0, keepdims=True), corr_ref.shape)


SMEM = pl.BlockSpec(memory_space=pltpu.SMEM)
VMEM = pl.BlockSpec(memory_space=pltpu.VMEM)


def call(kernel, name, outs, ins, scratch, micros, args):
    return pl.pallas_call(
        kernel,
        out_shape=outs,
        in_specs=ins,
        out_specs=jax.tree.map(lambda _: VMEM, outs),
        scratch_shapes=scratch,
        compiler_params=pltpu.CompilerParams(vmem_limit_bytes=16 << 20),
        cost_estimate=pl.CostEstimate(flops=0, bytes_accessed=int(micros * 3.5e6), transcendentals=0),
        name=name,
    )(*args)


def shape_of(dtype, *dims):
    return jax.ShapeDtypeStruct(dims, dtype)


def prepare(place, choice, peram):
    count = 3 * choice.shape[0]
    return call(
        prepare_kernel,
        "prepare",
        (
            shape_of(BF16, 2, 128, 64),
            shape_of(BF16, 2, 128, 128),
            shape_of(BF16, count, 128, 192),
            shape_of(BF16, count, 256, 128),
        ),
        [SMEM, SMEM, VMEM],
        [pltpu.VMEM((count, 64, 128), F32), pltpu.VMEM((HALF, 128), F32)],
        3,
        (place, choice, peram),
    )


def first_index(left_r, left_n, mine, theirs):
    return call(
        first_index_kernel,
        "first_index",
        shape_of(F32, HALF * 64, 128),
        [VMEM] * 4,
        [pltpu.VMEM((2 * HALF * HALF, 128), F32), pltpu.VMEM((HALF * STEPS, 128), F32)],
        5,
        (left_r, left_n, mine, theirs),
    )


def own_rows(place, inner):
    return call(rows_kernel, "own_rows", shape_of(F32, 2, 2, 64, 64), [SMEM, VMEM], [], 3, (place, inner))


def correlate(place, sink, flipped, full, inner, copies):
    return call(
        correlate_kernel,
        "correlate",
        shape_of(F32, copies, 128),
        [SMEM, VMEM, VMEM, VMEM, VMEM],
        [],
        4,
        (place, sink, flipped, full, inner),
    )


def swapped(value, axis, mask):
    count = lax.axis_size(axis)
    return lax.ppermute(value, axis, [(i, i ^ mask) for i in range(count)])


def shards(vectors, perambulators, shift_steps, spin_choice):
    vec = vectors[0]
    nvec = vec.shape[2]
    z_count, run_count = lax.axis_size("z"), lax.axis_size("z") * lax.axis_size("yl")
    space_count = run_count * lax.axis_size("core")
    combos = spin_choice.shape[0]
    factor = 1.0 / math.sqrt(24.0 * vec.shape[3] * space_count)
    corr_factor = 0.25 / (nvec * math.sqrt(nvec))
    core = lax.axis_index("core")
    run = lax.axis_index("z") * lax.axis_size("yl") + lax.axis_index("yl")
    peram = perambulators[0].reshape(-1, 2, nvec, nvec)

    away = pair_products((1 - core)[None], vec, factor)
    got = swapped(away, "core", 1)
    keep = pair_products(core[None], vec, factor)
    part = (keep + got).reshape(run_count, -1, 128)
    place = jnp.stack([core, run]).astype(jnp.int32)
    place, part = lax.optimization_barrier((place, part))
    spread = lax.all_to_all(part, ("z", "yl"), 0, 0, tiled=True)
    left_r, left_n, flipped, full = prepare(place, spin_choice, peram)
    spread, left_r = lax.optimization_barrier((spread, left_r))
    own = spread.sum(0)

    every = jnp.broadcast_to(own[None], (run_count,) + own.shape)
    near = jnp.stack([own, swapped(own, "yh", 1)])
    mine = lax.all_to_all(every, ("z", "yl"), 0, 0, tiled=True)
    side = swapped(near, "x", 1)
    mine, side = lax.optimization_barrier((mine, side))
    mine = mine.reshape(-1, 128)
    wider = jnp.concatenate([near, side])
    theirs = swapped(mine, "core", 1)
    inner = first_index(left_r, left_n, mine, theirs)
    last = swapped(wider, "x", 2)
    last, inner = lax.optimization_barrier((last, inner))
    all_times = jnp.concatenate([wider, last])
    now = lax.axis_index("yh") * lax.axis_size("x") + lax.axis_index("x")
    away_by = now ^ ((now + shift_steps[0]) % 8)
    pick = (away_by & 2) * 2 + (away_by & 1) * 2 + (away_by >> 2)
    sink = lax.dynamic_index_in_dim(all_times, pick, 0, keepdims=False)
    corr = correlate(place, sink, flipped, full, inner, space_count)
    total = lax.all_to_all(corr, ("z", "yl", "core"), 0, 0, tiled=True).sum(0)
    rows = own_rows(place, inner)
    correlator = jnp.transpose((total[: 2 * combos] * corr_factor).reshape(1, 2, combos), (0, 2, 1))
    return (rows.reshape(1, 2, 2, nvec * nvec)[0], correlator)


def solution(mesh):
    fine = Mesh(mesh.devices.reshape(2, 4, 8, 2, 2), ("yh", "x", "z", "yl", "core"))
    times, space = ("yh", "x"), ("z", "yl", "core")
    placed = (P(times, None, None, None, space), P(times, None, None, None), P(times), P())

    def whole(vectors, perambulators, shift_steps, spin_choice):
        rows, correlator = shards(vectors, perambulators, shift_steps, spin_choice)
        return rows[None], correlator

    return jax.shard_map(
        whole,
        mesh=fine,
        in_specs=placed,
        out_specs=(P(times, space, None, None), P(times, None, None)),
        check_vma=False,
    )
```

```python
import functools
import math

import jax
import jax.numpy as jnp
from jax import lax
from jax.experimental import pallas as pl
from jax.experimental.pallas import tpu as pltpu
from jax.sharding import Mesh
from jax.sharding import PartitionSpec as P

F32 = jnp.float32
BF16 = jnp.bfloat16
HALF = 32
STEPS = 16
LEAD = (1, 0, 2)
SMEM = pl.BlockSpec(memory_space=pltpu.SMEM)
VMEM = pl.BlockSpec(memory_space=pltpu.VMEM)


def split(value):
    high = value.astype(BF16)
    return high, (value - high.astype(F32)).astype(BF16)


def dot_nn(left, right):
    return lax.dot_general(left, right, (((1,), (0,)), ((), ())), preferred_element_type=F32)


def dot_nt(left, right):
    return lax.dot_general(left, right, (((1,), (1,)), ((), ())), preferred_element_type=F32)


def dot_tn(left, right):
    return lax.dot_general(left, right, (((0,), (0,)), ((), ())), preferred_element_type=F32)


def lanes_of(shape):
    return lax.broadcasted_iota(jnp.int32, shape, 1)


def pair_kernel(factor, half_ref, vec_ref, *refs):
    *so_far, out_ref, ext, lead, cross_high, cross_low = refs
    half = half_ref[0]
    own = pl.multiple_of(half * HALF, HALF)
    other = pl.multiple_of((1 - half) * HALF, HALF)
    for part in range(2):
        for colour in range(3):
            ext[part * 3 + colour, 0:HALF] = vec_ref[part, colour, pl.ds(own, HALF), :]
            ext[part * 3 + colour, HALF : HALF + STEPS] = vec_ref[part, colour, pl.ds(own, STEPS), :]
    sites = vec_ref.shape[3]
    for colour in range(3):
        at = colour * 2 * sites
        own_re, own_im = ext[colour, 0:HALF], ext[3 + colour, 0:HALF]
        oth_re = vec_ref[0, colour, pl.ds(other, HALF), :]
        oth_im = vec_ref[1, colour, pl.ds(other, HALF), :]
        for place, value in enumerate(
            (
                (own_re, -own_im),
                (own_im, own_re),
                (oth_re, -oth_im),
                (oth_im, oth_re),
            )
        ):
            for side in range(2):
                high, low = split(value[side])
                columns = slice(at + side * sites, at + (side + 1) * sites)
                lead[place * HALF : (place + 1) * HALF, columns] = high
                lead[128 + place * HALF : 128 + (place + 1) * HALF, columns] = low
    first, second = None, None
    for colour in range(3):
        one, two = (colour + 1) % 3, (colour + 2) % 3
        for step in range(1, STEPS + 1):
            here = slice((step - 1) * HALF, step * HALF)
            one_re, one_im = ext[one, 0:HALF], ext[3 + one, 0:HALF]
            two_re, two_im = ext[two, 0:HALF], ext[3 + two, 0:HALF]
            one_re2, one_im2 = ext[one, step : step + HALF], ext[3 + one, step : step + HALF]
            two_re2, two_im2 = ext[two, step : step + HALF], ext[3 + two, step : step + HALF]
            re = (one_re * two_re2 - one_im * two_im2) - (two_re * one_re2 - two_im * one_im2)
            im = (one_re * two_im2 + one_im * two_re2) - (two_re * one_im2 + two_im * one_re2)
            for side, value in enumerate((re, im)):
                high, low = split(value)
                columns = slice(side * sites, (side + 1) * sites)
                cross_high[colour, here, columns] = high
                cross_low[colour, here, columns] = low
        columns = slice(colour * 2 * sites, (colour + 1) * 2 * sites)
        more = dot_nt(cross_high[colour], lead[:, columns])
        first = more if first is None else first + more
        more = dot_nt(cross_low[colour], lead[0:128, columns])
        second = more if second is None else second + more
    total = (first[:, 0:128] + first[:, 128:256] + second) * (-factor)
    for step in range(STEPS):
        places = pl.ds(step, HALF, stride=STEPS)
        value = total[step * HALF : (step + 1) * HALF]
        out_ref[places, :] = value + so_far[0][places, :] if so_far else value


def pair_products(half, vec, factor, *so_far):
    sites = vec.shape[3]
    return pl.pallas_call(
        functools.partial(pair_kernel, factor),
        out_shape=jax.ShapeDtypeStruct((HALF * STEPS, 128), F32),
        in_specs=[SMEM] + [VMEM] * (1 + len(so_far)),
        out_specs=VMEM,
        scratch_shapes=[
            pltpu.VMEM((6, HALF + STEPS, sites), F32),
            pltpu.VMEM((256, 6 * sites), BF16),
            pltpu.VMEM((3, HALF * STEPS, 2 * sites), BF16),
            pltpu.VMEM((3, HALF * STEPS, 2 * sites), BF16),
        ],
        compiler_params=pltpu.CompilerParams(vmem_limit_bytes=10 << 20),
        name="pair_products",
    )(half, vec, *so_far)


def swap_parts(value):
    lane = lanes_of(value.shape)
    return jnp.where(lane % 64 < 32, pltpu.roll(value, 96, 1), pltpu.roll(value, 32, 1))


def turned(value, sign):
    return -swap_parts(value) * sign


def part_signs(shape):
    return jnp.where(lanes_of(shape) % 64 < 32, 1.0, -1.0)


def prepare_kernel(place_ref, choice_ref, peram_ref, left_r_ref, left_n_ref, flipped_ref, full_ref, quark, weights):
    core, run = place_ref[0], place_ref[1]
    first = core == 0
    combos = choice_ref.shape[0]
    plain = part_signs((64, 128))
    for s in range(combos):
        for q in range(3):
            spin = choice_ref[s, q]
            parts = []
            for part in range(2):
                top = peram_ref[spin, part, pl.ds(pl.multiple_of(core * HALF, HALF), HALF), :]
                low = peram_ref[spin, part, pl.ds(pl.multiple_of((1 - core) * HALF, HALF), HALF), :]
                both = jnp.concatenate([top, low], axis=0)
                left, right = both[:, 0:HALF], both[:, HALF : 2 * HALF]
                parts.append((jnp.where(first, left, right), jnp.where(first, right, left)))
            (re_own, re_oth), (im_own, im_oth) = parts
            value = jnp.concatenate([re_own, im_own, re_oth, im_oth], axis=1)
            quark[s * 3 + q] = value
            high, low = split(value.T)
            flipped_ref[s, q * 128 : (q + 1) * 128] = jnp.concatenate([high, high, low], axis=1)
            full_high, full_low = split(jnp.concatenate([value * plain, swap_parts(value)], axis=0))
            full_ref[s * 3 + q, 0:128] = jnp.concatenate([full_high, full_high], axis=1)
            full_ref[s * 3 + q, 128:256] = jnp.concatenate([full_low, jnp.zeros_like(full_low)], axis=1)

    for s in range(combos):
        for slot in range(3):
            for e in range(2):
                row = s * 6 + slot * 2 + e
                weights[row : row + 1] = quark[s * 3 + LEAD[slot], pl.ds(2 * run + e, 1), :]
    tail = 6 * combos
    shape = (HALF - tail, 128)
    lane, row = lanes_of(shape), lax.broadcasted_iota(jnp.int32, shape, 0)
    number = 4 * run + 2 * core + row
    in_own = (number >= HALF) == (core == 1)
    lit = (number % HALF + jnp.where(in_own, 0, 64)) == lane
    weights[tail:HALF] = jnp.where(lit & (row < 2), 1.0, 0.0)

    lead = weights[...]
    sign = part_signs((HALF, 128))
    lead_high, lead_low = split(lead)
    conj_high, conj_low = split(lead * sign)
    cross_high, cross_low = split(swap_parts(lead))
    blank = jnp.zeros((HALF, 64), BF16)
    for g in range(2):
        re, im = slice(g * 64, g * 64 + 32), slice(g * 64 + 32, g * 64 + 64)
        there = slice(64 - g * 64, 128 - g * 64)
        none = jnp.zeros((HALF, 32), BF16)
        for k, rows in enumerate(
            (
                (-lead_high[:, re], -lead_high[:, re]),
                (-lead_high[:, im], -lead_high[:, im]),
                (-lead_low[:, re], none),
                (-lead_low[:, im], none),
            )
        ):
            left_r_ref[g, k * HALF : (k + 1) * HALF] = jnp.concatenate(rows, axis=1)
        for k, (rows, low_rows) in enumerate(
            (
                (conj_high[:, there], conj_high[:, there]),
                (cross_high[:, there], cross_high[:, there]),
                (conj_low[:, there], blank),
                (cross_low[:, there], blank),
            )
        ):
            left_n_ref[g, k * HALF : (k + 1) * HALF] = jnp.concatenate([rows, low_rows], axis=1)


def first_index_kernel(g, left_r_ref, left_n_ref, from_ref, inner, picked_ref, pairs, *turned_refs):
    if g == 1:
        (turned_ref,) = turned_refs
        turned_ref[...] = pltpu.roll(from_ref[...], 64, 1)
        from_ref = turned_ref
    pairs[pl.ds(0, HALF, stride=HALF + 1), :] = jnp.zeros((HALF, 128), F32)
    for j in range(HALF):
        straight = min(STEPS, HALF - 1 - j)
        at = j * HALF
        if straight:
            pairs[at + j + 1 : at + j + 1 + straight] = from_ref[j * STEPS : j * STEPS + straight]
        if straight < STEPS:
            pairs[at : at + STEPS - straight] = from_ref[j * STEPS + straight : (j + 1) * STEPS]
    for j in range(HALF):
        count = STEPS - 1
        straight = min(count, HALF - 1 - j)
        if straight:
            pairs[pl.ds((j + 1) * HALF + j, straight, stride=HALF), :] = -from_ref[j * STEPS : j * STEPS + straight]
        if straight < count:
            pairs[pl.ds(j, count - straight, stride=HALF), :] = -from_ref[j * STEPS + straight : j * STEPS + count]

    wide = lanes_of((HALF, 128))
    sign = part_signs((HALF, 128))
    left_r, left_n = left_r_ref[g], left_n_ref[g]
    here = g * 64
    for b in range(0, HALF, 4):
        stacks, packs = [], []
        for e in range(4):
            at = (b + e) * HALF
            value = pairs[at : at + HALF]
            high = value.astype(BF16)
            full = high.astype(F32)
            low = value - full
            stacks.append(jnp.concatenate([high, low.astype(BF16)], axis=0))
            if g == 0:
                full = pltpu.roll(full, 64, 1)
            else:
                low = pltpu.roll(low, 64, 1)
            packs.append(jnp.where(wide < 64, full, low).astype(BF16))
        more = dot_nt(left_n, jnp.concatenate(packs, axis=0))
        more_re = more[0:HALF] + more[2 * HALF : 3 * HALF]
        more_im = more[HALF : 2 * HALF] + more[3 * HALF : 4 * HALF]
        for pair in range(2):
            some = dot_nn(left_r, jnp.concatenate(stacks[2 * pair : 2 * pair + 2], axis=1))
            some_re = some[0:HALF] + some[2 * HALF : 3 * HALF]
            some_im = some[HALF : 2 * HALF] + some[3 * HALF : 4 * HALF]
            for e in range(2):
                at = (2 * pair + e) * 32
                columns = slice(e * 128, e * 128 + 128)
                result = some_re[:, columns] + turned(some_im[:, columns], sign)
                extra_re, extra_im = more_re, more_im
                if (here - at) % 128:
                    extra_re = pltpu.roll(extra_re, (here - at) % 128, 1)
                if (here + 32 - at) % 128:
                    extra_im = pltpu.roll(extra_im, (here + 32 - at) % 128, 1)
                extra = jnp.where(wide % 64 < 32, extra_re, extra_im)
                result += jnp.where((wide < 64) == (g == 0), extra, 0.0)
                inner[pl.ds(b + 2 * pair + e, HALF, stride=HALF), :] = result
    picked_ref[...] = inner[(HALF - 8) * HALF : (HALF - 6) * HALF]


def rows_kernel(place_ref, picked_ref, picked2_ref, rows_ref):
    first = place_ref[0] == 0
    for e in range(2):
        at = slice(e * HALF, (e + 1) * HALF)
        value = jnp.concatenate([picked_ref[at], picked2_ref[at]], axis=0)
        shape = (64, 64)
        mixed = (lax.broadcasted_iota(jnp.int32, shape, 0) < HALF) != (lanes_of(shape) < HALF)
        for part in range(2):
            one = jnp.concatenate(
                [value[:, part * 32 : part * 32 + 32], value[:, 64 + part * 32 : 96 + part * 32]], axis=1
            )
            one = one - jnp.where(mixed, one, 0.0).T
            top = jnp.where(first, one[0:HALF], one[HALF:64])
            low = jnp.where(first, one[HALF:64], one[0:HALF])
            both = jnp.concatenate([top, low], axis=0)
            left, right = both[:, 0:HALF], both[:, HALF:64]
            rows_ref[e, part] = jnp.concatenate(
                [jnp.where(first, left, right), jnp.where(first, right, left)], axis=1
            )


def correlate_kernel(place_ref, flipped_ref, full_ref, inner_ref, inner2_ref, sink_ref, corr_ref):
    run = place_ref[1]
    combos = flipped_ref.shape[0]
    shape = (STEPS, 128)
    step = lax.broadcasted_iota(jnp.int32, shape, 0)
    share = jnp.where(lanes_of(shape) < 64, 1.0 / 3.0, 1.0) * jnp.where(step == STEPS - 1, 0.5, 1.0)
    sink = []
    for e in range(2):
        shape = (HALF, STEPS)
        target = (2 * run + e + lanes_of(shape) + 1) % HALF
        move = jnp.where(lax.broadcasted_iota(jnp.int32, shape, 0) == target, 1.0, 0.0).astype(BF16)
        high, low = split(sink_ref[e * STEPS : (e + 1) * STEPS] * share)
        placed = dot_nn(move, high) + dot_nn(move, low)
        for part in range(2):
            one = jnp.concatenate(
                [placed[:, part * 32 : part * 32 + 32], placed[:, 64 + part * 32 : 96 + part * 32]], axis=1
            )
            one = jnp.concatenate([one, jnp.zeros((HALF, 64), F32)], axis=0)
            sink.append(one - one.T)
    sink_high, sink_low = split(jnp.concatenate(sink, axis=1))
    sink_stack = jnp.concatenate([sink_high, sink_low, sink_high], axis=0)

    shape = (128, 128)
    row, lane = lax.broadcasted_iota(jnp.int32, shape, 0), lanes_of(shape)
    cross = (row < 64) != (lane < 64)
    side = jnp.where(lanes_of((64, 128)) < 64, 1.0, -1.0)
    results = []
    for s in range(combos):
        dual = []
        whole = dot_nn(flipped_ref[s], sink_stack)
        for q in range(3):
            out = whole[q * 128 : (q + 1) * 128]
            re = jnp.concatenate([out[0:32], out[64:96]], axis=0)
            im = jnp.concatenate([out[32:64], out[96:128]], axis=0)
            per_row = []
            for e in range(2):
                re_e, im_e = re[:, e * 128 : (e + 1) * 128], im[:, e * 128 : (e + 1) * 128]
                per_row.append(
                    (
                        re_e + pltpu.roll(im_e, 64, 1) * side,
                        im_e - pltpu.roll(re_e, 64, 1) * side,
                    )
                )
            dual.append(per_row)
        blocks = []
        for slot in range(3):
            at = slice((s * 6 + slot * 2) * HALF, (s * 6 + slot * 2 + 2) * HALF)
            blocks.append(jnp.concatenate([inner_ref[at], inner2_ref[at]], axis=0))
        masked = [jnp.where(cross, block, 0.0) for block in blocks]
        acc_re, acc_im = jnp.zeros((HALF, 128), F32), jnp.zeros((HALF, 128), F32)
        for q, lefts, partners in (
            (2, (blocks[0], blocks[1]), (0, 1)),
            (1, (blocks[2], masked[1]), (0, 2)),
            (0, (masked[0], masked[2]), (2, 1)),
        ):
            high, low = split(jnp.concatenate(lefts, axis=0))
            out = dot_nt(jnp.concatenate([high, low], axis=1), full_ref[s * 3 + q])
            out = out[:, 0:128] + out[:, 128:256]
            for k in range(2):
                for g in range(2):
                    for e in range(2):
                        at = k * 128 + g * 64 + e * HALF
                        part = out[at : at + HALF]
                        half = slice(g * HALF, (g + 1) * HALF)
                        acc_re += part * dual[partners[k]][e][0][half]
                        acc_im += part * dual[partners[k]][e][1][half]
        results.append((jnp.sum(acc_re, axis=0, keepdims=True), jnp.sum(acc_im, axis=0, keepdims=True)))
    shape = (combos, 128)
    diagonal = lax.broadcasted_iota(jnp.int32, shape, 0) == lanes_of(shape)
    both = []
    for part in range(2):
        table = jnp.sum(jnp.concatenate([result[part] for result in results], axis=0), axis=1, keepdims=True)
        both.append(jnp.sum(jnp.where(diagonal, table, 0.0), axis=0, keepdims=True))
    corr_ref[...] = jnp.broadcast_to(jnp.concatenate(both, axis=0)[None], corr_ref.shape)


def call(kernel, name, outs, ins, scratch, micros, args):
    return pl.pallas_call(
        kernel,
        out_shape=outs,
        in_specs=ins,
        out_specs=jax.tree.map(lambda _: VMEM, outs),
        scratch_shapes=scratch,
        compiler_params=pltpu.CompilerParams(vmem_limit_bytes=6 << 20),
        cost_estimate=pl.CostEstimate(flops=int(micros * 1e9), bytes_accessed=0, transcendentals=0),
        name=name,
    )(*args)


def shape_of(dtype, *dims):
    return jax.ShapeDtypeStruct(dims, dtype)


def prepare(place, choice, peram):
    count = 3 * choice.shape[0]
    return call(
        prepare_kernel,
        "prepare",
        (
            shape_of(BF16, 2, 128, 64),
            shape_of(BF16, 2, 128, 128),
            shape_of(BF16, count // 3, 384, 192),
            shape_of(BF16, count, 256, 256),
        ),
        [SMEM, SMEM, VMEM],
        [pltpu.VMEM((count, 64, 128), F32), pltpu.VMEM((HALF, 128), F32)],
        3,
        (place, choice, peram),
    )


def sum_kernel(parts_ref, own_ref, every_ref):
    own = parts_ref[0]
    for k in range(1, parts_ref.shape[0]):
        own += parts_ref[k]
    own_ref[...] = own
    for k in range(parts_ref.shape[0]):
        every_ref[k] = own


def sum_parts(parts):
    outs = (shape_of(F32, *parts.shape[1:]), shape_of(F32, *parts.shape))
    return call(sum_kernel, "sum_parts", outs, [VMEM], [], 0.2, (parts,))


def first_index(g, left_r, left_n, half):
    scratch = [pltpu.VMEM((HALF * HALF, 128), F32)]
    if g == 1:
        scratch.append(pltpu.VMEM((HALF * STEPS, 128), F32))
    return call(
        functools.partial(first_index_kernel, g),
        "first_index",
        (shape_of(F32, HALF * HALF, 128), shape_of(F32, 2 * HALF, 128)),
        [VMEM] * 3,
        scratch,
        2,
        (left_r, left_n, half),
    )


def own_rows(place, picked):
    return call(rows_kernel, "own_rows", shape_of(F32, 2, 2, 64, 64), [SMEM, VMEM, VMEM], [], 3, (place, *picked))


def correlate(place, flipped, full, inner, sink, copies):
    return call(
        correlate_kernel,
        "correlate",
        shape_of(F32, copies, 2, 128),
        [SMEM] + [VMEM] * 5,
        [],
        3,
        (place, flipped, full, *inner, sink),
    )


def swapped(value, axis, mask):
    count = lax.axis_size(axis)
    return lax.ppermute(value, axis, [(i, i ^ mask) for i in range(count)])


def shards(vectors, perambulators, shift_steps, spin_choice):
    vec = vectors[0]
    nvec = vec.shape[2]
    z_count, run_count = lax.axis_size("z"), lax.axis_size("z") * lax.axis_size("yl")
    space_count = run_count * lax.axis_size("core")
    combos = spin_choice.shape[0]
    factor = 1.0 / math.sqrt(24.0 * vec.shape[3] * space_count)
    corr_factor = 0.25 / (nvec * math.sqrt(nvec))
    core = lax.axis_index("core")
    run = lax.axis_index("z") * lax.axis_size("yl") + lax.axis_index("yl")
    peram = perambulators[0].reshape(-1, 2, nvec, nvec)

    beside = swapped(vec, "core", 1)
    part = pair_products(core[None], vec, factor)
    part = pair_products(core[None], beside, factor, part).reshape(run_count, -1, 128)
    time_count = lax.axis_size("yh") * lax.axis_size("x")
    now = lax.axis_index("yh") * lax.axis_size("x") + lax.axis_index("x")
    away_by = now ^ ((now + shift_steps[0]) % time_count)
    pick = (away_by & 1) * 4 + (away_by & 2) + (away_by >> 2)
    place = jnp.stack([core, run]).astype(jnp.int32)
    place, pick, part = lax.optimization_barrier((place, pick, part))
    spread = lax.all_to_all(part, ("z", "yl"), 0, 0, tiled=True)
    left_r, left_n, flipped, full = prepare(place, spin_choice, peram)
    spread, left_r = lax.optimization_barrier((spread, left_r))
    own, every = sum_parts(spread)

    one = swapped(own, "yh", 1)
    near = jnp.stack([own, one])
    two = swapped(near, "x", 2)
    wider = jnp.concatenate([near, two])
    four = swapped(wider, "x", 1)
    mine = lax.all_to_all(every, ("z", "yl"), 0, 0, tiled=True)
    mine, _ = lax.optimization_barrier((mine, two))
    mine = mine.reshape(-1, 128)
    theirs = swapped(mine, "core", 1)
    inner, picked = zip(first_index(0, left_r, left_n, mine), first_index(1, left_r, left_n, theirs), strict=True)
    four, inner = lax.optimization_barrier((four, inner))
    sink = lax.dynamic_index_in_dim(jnp.concatenate([wider, four]), pick, 0, keepdims=False)
    corr = correlate(place, flipped, full, inner, sink, space_count)
    total = lax.all_to_all(corr, ("z", "yl", "core"), 0, 0, tiled=True).sum(0)
    rows = own_rows(place, picked)
    correlator = jnp.transpose((total[:, :combos] * corr_factor)[None], (0, 2, 1))
    return (rows.reshape(1, 2, 2, nvec * nvec)[0], correlator)


def solution(mesh):
    fine = Mesh(mesh.devices.reshape(2, 4, 8, 2, 2), ("yh", "x", "z", "yl", "core"))
    times, space = ("yh", "x"), ("z", "yl", "core")
    placed = (P(times, None, None, None, space), P(times, None, None, None), P(times), P())

    def whole(vectors, perambulators, shift_steps, spin_choice):
        rows, correlator = shards(vectors, perambulators, shift_steps, spin_choice)
        return rows[None], correlator

    return jax.shard_map(
        whole,
        mesh=fine,
        in_specs=placed,
        out_specs=(P(times, space, None, None), P(times, None, None)),
        check_vma=False,
    )
```

```python
import functools
import math

import jax
import jax.numpy as jnp
from jax import lax
from jax.experimental import pallas as pl
from jax.experimental.pallas import tpu as pltpu
from jax.sharding import Mesh
from jax.sharding import PartitionSpec as P

F32 = jnp.float32
BF16 = jnp.bfloat16
HALF = 32
STEPS = 16
LEAD = (1, 0, 2)
SMEM = pl.BlockSpec(memory_space=pltpu.SMEM)
VMEM = pl.BlockSpec(memory_space=pltpu.VMEM)


def split(value):
    high = value.astype(BF16)
    return high, (value - high.astype(F32)).astype(BF16)


def dot_nn(left, right):
    return lax.dot_general(left, right, (((1,), (0,)), ((), ())), preferred_element_type=F32)


def dot_nt(left, right):
    return lax.dot_general(left, right, (((1,), (1,)), ((), ())), preferred_element_type=F32)


def dot_tn(left, right):
    return lax.dot_general(left, right, (((0,), (0,)), ((), ())), preferred_element_type=F32)


def lanes_of(shape):
    return lax.broadcasted_iota(jnp.int32, shape, 1)


def pair_kernel(factor, half_ref, vec_ref, *refs):
    *so_far, out_ref, ext, lead, cross_high, cross_low = refs
    half = half_ref[0]
    own = pl.multiple_of(half * HALF, HALF)
    other = pl.multiple_of((1 - half) * HALF, HALF)
    for part in range(2):
        for colour in range(3):
            ext[part * 3 + colour, 0:HALF] = vec_ref[part, colour, pl.ds(own, HALF), :]
            ext[part * 3 + colour, HALF : HALF + STEPS] = vec_ref[part, colour, pl.ds(own, STEPS), :]
    sites = vec_ref.shape[3]
    for colour in range(3):
        at = colour * 2 * sites
        own_re, own_im = ext[colour, 0:HALF], ext[3 + colour, 0:HALF]
        oth_re = vec_ref[0, colour, pl.ds(other, HALF), :]
        oth_im = vec_ref[1, colour, pl.ds(other, HALF), :]
        for place, value in enumerate(
            (
                (own_re, -own_im),
                (own_im, own_re),
                (oth_re, -oth_im),
                (oth_im, oth_re),
            )
        ):
            for side in range(2):
                high, low = split(value[side])
                columns = slice(at + side * sites, at + (side + 1) * sites)
                lead[place * HALF : (place + 1) * HALF, columns] = high
                lead[128 + place * HALF : 128 + (place + 1) * HALF, columns] = low
    first, second = None, None
    for colour in range(3):
        one, two = (colour + 1) % 3, (colour + 2) % 3
        for step in range(1, STEPS + 1):
            here = slice((step - 1) * HALF, step * HALF)
            one_re, one_im = ext[one, 0:HALF], ext[3 + one, 0:HALF]
            two_re, two_im = ext[two, 0:HALF], ext[3 + two, 0:HALF]
            one_re2, one_im2 = ext[one, step : step + HALF], ext[3 + one, step : step + HALF]
            two_re2, two_im2 = ext[two, step : step + HALF], ext[3 + two, step : step + HALF]
            re = (one_re * two_re2 - one_im * two_im2) - (two_re * one_re2 - two_im * one_im2)
            im = (one_re * two_im2 + one_im * two_re2) - (two_re * one_im2 + two_im * one_re2)
            for side, value in enumerate((re, im)):
                high, low = split(value)
                columns = slice(side * sites, (side + 1) * sites)
                cross_high[colour, here, columns] = high
                cross_low[colour, here, columns] = low
        columns = slice(colour * 2 * sites, (colour + 1) * 2 * sites)
        more = dot_nt(cross_high[colour], lead[:, columns])
        first = more if first is None else first + more
        more = dot_nt(cross_low[colour], lead[0:128, columns])
        second = more if second is None else second + more
    total = (first[:, 0:128] + first[:, 128:256] + second) * (-factor)
    for step in range(STEPS):
        places = pl.ds(step, HALF, stride=STEPS)
        value = total[step * HALF : (step + 1) * HALF]
        out_ref[places, :] = value + so_far[0][places, :] if so_far else value


def pair_products(half, vec, factor, *so_far):
    sites = vec.shape[3]
    return pl.pallas_call(
        functools.partial(pair_kernel, factor),
        out_shape=jax.ShapeDtypeStruct((HALF * STEPS, 128), F32),
        in_specs=[SMEM] + [VMEM] * (1 + len(so_far)),
        out_specs=VMEM,
        scratch_shapes=[
            pltpu.VMEM((6, HALF + STEPS, sites), F32),
            pltpu.VMEM((256, 6 * sites), BF16),
            pltpu.VMEM((3, HALF * STEPS, 2 * sites), BF16),
            pltpu.VMEM((3, HALF * STEPS, 2 * sites), BF16),
        ],
        compiler_params=pltpu.CompilerParams(vmem_limit_bytes=10 << 20),
        name="pair_products",
    )(half, vec, *so_far)


def swap_parts(value):
    lane = lanes_of(value.shape)
    return jnp.where(lane % 64 < 32, pltpu.roll(value, 96, 1), pltpu.roll(value, 32, 1))


def turned(value, sign):
    return -swap_parts(value) * sign


def part_signs(shape):
    return jnp.where(lanes_of(shape) % 64 < 32, 1.0, -1.0)


def prepare_kernel(place_ref, choice_ref, peram_ref, left_r_ref, left_n_ref, flipped_ref, full_ref, quark, weights):
    core, run = place_ref[0], place_ref[1]
    first = core == 0
    combos = choice_ref.shape[0]
    plain = part_signs((64, 128))
    for s in range(combos):
        for q in range(3):
            spin = choice_ref[s, q]
            parts = []
            for part in range(2):
                top = peram_ref[spin, part, pl.ds(pl.multiple_of(core * HALF, HALF), HALF), :]
                low = peram_ref[spin, part, pl.ds(pl.multiple_of((1 - core) * HALF, HALF), HALF), :]
                both = jnp.concatenate([top, low], axis=0)
                left, right = both[:, 0:HALF], both[:, HALF : 2 * HALF]
                parts.append((jnp.where(first, left, right), jnp.where(first, right, left)))
            (re_own, re_oth), (im_own, im_oth) = parts
            value = jnp.concatenate([re_own, im_own, re_oth, im_oth], axis=1)
            quark[s * 3 + q] = value
            high, low = split(value.T)
            flipped_ref[s, q * 128 : (q + 1) * 128] = jnp.concatenate([high, high, low], axis=1)
            full_high, full_low = split(jnp.concatenate([value * plain, swap_parts(value)], axis=0))
            full_ref[s * 3 + q, 0:128] = jnp.concatenate([full_high, full_high], axis=1)
            full_ref[s * 3 + q, 128:256] = jnp.concatenate([full_low, jnp.zeros_like(full_low)], axis=1)

    for s in range(combos):
        for slot in range(3):
            for e in range(2):
                row = s * 6 + slot * 2 + e
                weights[row : row + 1] = quark[s * 3 + LEAD[slot], pl.ds(2 * run + e, 1), :]
    tail = 6 * combos
    shape = (HALF - tail, 128)
    lane, row = lanes_of(shape), lax.broadcasted_iota(jnp.int32, shape, 0)
    number = 4 * run + 2 * core + row
    in_own = (number >= HALF) == (core == 1)
    lit = (number % HALF + jnp.where(in_own, 0, 64)) == lane
    weights[tail:HALF] = jnp.where(lit & (row < 2), 1.0, 0.0)

    lead = weights[...]
    sign = part_signs((HALF, 128))
    lead_high, lead_low = split(lead)
    conj_high, conj_low = split(lead * sign)
    cross_high, cross_low = split(swap_parts(lead))
    blank = jnp.zeros((HALF, 64), BF16)
    for g in range(2):
        re, im = slice(g * 64, g * 64 + 32), slice(g * 64 + 32, g * 64 + 64)
        there = slice(64 - g * 64, 128 - g * 64)
        none = jnp.zeros((HALF, 32), BF16)
        for k, rows in enumerate(
            (
                (-lead_high[:, re], -lead_high[:, re]),
                (-lead_high[:, im], -lead_high[:, im]),
                (-lead_low[:, re], none),
                (-lead_low[:, im], none),
            )
        ):
            left_r_ref[g, k * HALF : (k + 1) * HALF] = jnp.concatenate(rows, axis=1)
        for k, (rows, low_rows) in enumerate(
            (
                (conj_high[:, there], conj_high[:, there]),
                (cross_high[:, there], cross_high[:, there]),
                (conj_low[:, there], blank),
                (cross_low[:, there], blank),
            )
        ):
            left_n_ref[g, k * HALF : (k + 1) * HALF] = jnp.concatenate([rows, low_rows], axis=1)


def first_index_kernel(g, left_r_ref, left_n_ref, from_ref, inner, picked_ref, pairs, *turned_refs):
    if g == 1:
        (turned_ref,) = turned_refs
        turned_ref[...] = pltpu.roll(from_ref[...], 64, 1)
        from_ref = turned_ref
    pairs[pl.ds(0, HALF, stride=HALF + 1), :] = jnp.zeros((HALF, 128), F32)
    for j in range(HALF):
        straight = min(STEPS, HALF - 1 - j)
        at = j * HALF
        if straight:
            pairs[at + j + 1 : at + j + 1 + straight] = from_ref[j * STEPS : j * STEPS + straight]
        if straight < STEPS:
            pairs[at : at + STEPS - straight] = from_ref[j * STEPS + straight : (j + 1) * STEPS]
    for j in range(HALF):
        count = STEPS - 1
        straight = min(count, HALF - 1 - j)
        if straight:
            pairs[pl.ds((j + 1) * HALF + j, straight, stride=HALF), :] = -from_ref[j * STEPS : j * STEPS + straight]
        if straight < count:
            pairs[pl.ds(j, count - straight, stride=HALF), :] = -from_ref[j * STEPS + straight : j * STEPS + count]

    wide = lanes_of((HALF, 128))
    sign = part_signs((HALF, 128))
    left_r, left_n = left_r_ref[g], left_n_ref[g]
    here = g * 64
    for b in range(0, HALF, 4):
        stacks, packs = [], []
        for e in range(4):
            at = (b + e) * HALF
            value = pairs[at : at + HALF]
            high = value.astype(BF16)
            full = high.astype(F32)
            low = value - full
            stacks.append(jnp.concatenate([high, low.astype(BF16)], axis=0))
            if g == 0:
                full = pltpu.roll(full, 64, 1)
            else:
                low = pltpu.roll(low, 64, 1)
            packs.append(jnp.where(wide < 64, full, low).astype(BF16))
        more = dot_nt(left_n, jnp.concatenate(packs, axis=0))
        more_re = more[0:HALF] + more[2 * HALF : 3 * HALF]
        more_im = more[HALF : 2 * HALF] + more[3 * HALF : 4 * HALF]
        for pair in range(2):
            some = dot_nn(left_r, jnp.concatenate(stacks[2 * pair : 2 * pair + 2], axis=1))
            some_re = some[0:HALF] + some[2 * HALF : 3 * HALF]
            some_im = some[HALF : 2 * HALF] + some[3 * HALF : 4 * HALF]
            for e in range(2):
                at = (2 * pair + e) * 32
                columns = slice(e * 128, e * 128 + 128)
                result = some_re[:, columns] + turned(some_im[:, columns], sign)
                extra_re, extra_im = more_re, more_im
                if (here - at) % 128:
                    extra_re = pltpu.roll(extra_re, (here - at) % 128, 1)
                if (here + 32 - at) % 128:
                    extra_im = pltpu.roll(extra_im, (here + 32 - at) % 128, 1)
                extra = jnp.where(wide % 64 < 32, extra_re, extra_im)
                result += jnp.where((wide < 64) == (g == 0), extra, 0.0)
                inner[pl.ds(b + 2 * pair + e, HALF, stride=HALF), :] = result
    picked_ref[...] = inner[(HALF - 8) * HALF : (HALF - 6) * HALF]


def rows_kernel(place_ref, picked_ref, picked2_ref, rows_ref):
    first = place_ref[0] == 0
    for e in range(2):
        at = slice(e * HALF, (e + 1) * HALF)
        value = jnp.concatenate([picked_ref[at], picked2_ref[at]], axis=0)
        shape = (64, 64)
        mixed = (lax.broadcasted_iota(jnp.int32, shape, 0) < HALF) != (lanes_of(shape) < HALF)
        for part in range(2):
            one = jnp.concatenate(
                [value[:, part * 32 : part * 32 + 32], value[:, 64 + part * 32 : 96 + part * 32]], axis=1
            )
            one = one - jnp.where(mixed, one, 0.0).T
            top = jnp.where(first, one[0:HALF], one[HALF:64])
            low = jnp.where(first, one[HALF:64], one[0:HALF])
            both = jnp.concatenate([top, low], axis=0)
            left, right = both[:, 0:HALF], both[:, HALF:64]
            rows_ref[e, part] = jnp.concatenate(
                [jnp.where(first, left, right), jnp.where(first, right, left)], axis=1
            )


def correlate_kernel(place_ref, flipped_ref, full_ref, inner_ref, inner2_ref, sink_ref, corr_ref):
    run = place_ref[1]
    combos = flipped_ref.shape[0]
    shape = (STEPS, 128)
    step = lax.broadcasted_iota(jnp.int32, shape, 0)
    share = jnp.where(lanes_of(shape) < 64, 1.0 / 3.0, 1.0) * jnp.where(step == STEPS - 1, 0.5, 1.0)
    sink = []
    for e in range(2):
        shape = (HALF, STEPS)
        target = (2 * run + e + lanes_of(shape) + 1) % HALF
        move = jnp.where(lax.broadcasted_iota(jnp.int32, shape, 0) == target, 1.0, 0.0).astype(BF16)
        high, low = split(sink_ref[e * STEPS : (e + 1) * STEPS] * share)
        placed = dot_nn(move, high) + dot_nn(move, low)
        for part in range(2):
            one = jnp.concatenate(
                [placed[:, part * 32 : part * 32 + 32], placed[:, 64 + part * 32 : 96 + part * 32]], axis=1
            )
            one = jnp.concatenate([one, jnp.zeros((HALF, 64), F32)], axis=0)
            sink.append(one - one.T)
    sink_high, sink_low = split(jnp.concatenate(sink, axis=1))
    sink_stack = jnp.concatenate([sink_high, sink_low, sink_high], axis=0)

    shape = (128, 128)
    row, lane = lax.broadcasted_iota(jnp.int32, shape, 0), lanes_of(shape)
    cross = (row < 64) != (lane < 64)
    side = jnp.where(lanes_of((64, 128)) < 64, 1.0, -1.0)
    results = []
    for s in range(combos):
        dual = []
        whole = dot_nn(flipped_ref[s], sink_stack)
        for q in range(3):
            out = whole[q * 128 : (q + 1) * 128]
            re = jnp.concatenate([out[0:32], out[64:96]], axis=0)
            im = jnp.concatenate([out[32:64], out[96:128]], axis=0)
            per_row = []
            for e in range(2):
                re_e, im_e = re[:, e * 128 : (e + 1) * 128], im[:, e * 128 : (e + 1) * 128]
                per_row.append(
                    (
                        re_e + pltpu.roll(im_e, 64, 1) * side,
                        im_e - pltpu.roll(re_e, 64, 1) * side,
                    )
                )
            dual.append(per_row)
        blocks = []
        for slot in range(3):
            at = slice((s * 6 + slot * 2) * HALF, (s * 6 + slot * 2 + 2) * HALF)
            blocks.append(jnp.concatenate([inner_ref[at], inner2_ref[at]], axis=0))
        masked = [jnp.where(cross, block, 0.0) for block in blocks]
        acc_re, acc_im = jnp.zeros((HALF, 128), F32), jnp.zeros((HALF, 128), F32)
        for q, lefts, partners in (
            (2, (blocks[0], blocks[1]), (0, 1)),
            (1, (blocks[2], masked[1]), (0, 2)),
            (0, (masked[0], masked[2]), (2, 1)),
        ):
            high, low = split(jnp.concatenate(lefts, axis=0))
            out = dot_nt(jnp.concatenate([high, low], axis=1), full_ref[s * 3 + q])
            out = out[:, 0:128] + out[:, 128:256]
            for k in range(2):
                for g in range(2):
                    for e in range(2):
                        at = k * 128 + g * 64 + e * HALF
                        part = out[at : at + HALF]
                        half = slice(g * HALF, (g + 1) * HALF)
                        acc_re += part * dual[partners[k]][e][0][half]
                        acc_im += part * dual[partners[k]][e][1][half]
        results.append((jnp.sum(acc_re, axis=0, keepdims=True), jnp.sum(acc_im, axis=0, keepdims=True)))
    shape = (combos, 128)
    diagonal = lax.broadcasted_iota(jnp.int32, shape, 0) == lanes_of(shape)
    both = []
    for part in range(2):
        table = jnp.sum(jnp.concatenate([result[part] for result in results], axis=0), axis=1, keepdims=True)
        both.append(jnp.sum(jnp.where(diagonal, table, 0.0), axis=0, keepdims=True))
    corr_ref[...] = jnp.broadcast_to(jnp.concatenate(both, axis=0)[None], corr_ref.shape)


def call(kernel, name, outs, ins, scratch, micros, args):
    return pl.pallas_call(
        kernel,
        out_shape=outs,
        in_specs=ins,
        out_specs=jax.tree.map(lambda _: VMEM, outs),
        scratch_shapes=scratch,
        compiler_params=pltpu.CompilerParams(vmem_limit_bytes=6 << 20),
        cost_estimate=pl.CostEstimate(flops=int(micros * 1e9), bytes_accessed=0, transcendentals=0),
        name=name,
    )(*args)


def shape_of(dtype, *dims):
    return jax.ShapeDtypeStruct(dims, dtype)


def prepare(place, choice, peram):
    count = 3 * choice.shape[0]
    return call(
        prepare_kernel,
        "prepare",
        (
            shape_of(BF16, 2, 128, 64),
            shape_of(BF16, 2, 128, 128),
            shape_of(BF16, count // 3, 384, 192),
            shape_of(BF16, count, 256, 256),
        ),
        [SMEM, SMEM, VMEM],
        [pltpu.VMEM((count, 64, 128), F32), pltpu.VMEM((HALF, 128), F32)],
        3,
        (place, choice, peram),
    )


def sum_kernel(parts_ref, own_ref, every_ref):
    own = parts_ref[0]
    for k in range(1, parts_ref.shape[0]):
        own += parts_ref[k]
    own_ref[...] = own
    for k in range(parts_ref.shape[0]):
        every_ref[k] = own


def sum_parts(parts):
    outs = (shape_of(F32, *parts.shape[1:]), shape_of(F32, *parts.shape))
    return call(sum_kernel, "sum_parts", outs, [VMEM], [], 0.2, (parts,))


def first_index(g, left_r, left_n, half):
    scratch = [pltpu.VMEM((HALF * HALF, 128), F32)]
    if g == 1:
        scratch.append(pltpu.VMEM((HALF * STEPS, 128), F32))
    return call(
        functools.partial(first_index_kernel, g),
        "first_index",
        (shape_of(F32, HALF * HALF, 128), shape_of(F32, 2 * HALF, 128)),
        [VMEM] * 3,
        scratch,
        2,
        (left_r, left_n, half),
    )


def own_rows(place, picked):
    return call(rows_kernel, "own_rows", shape_of(F32, 2, 2, 64, 64), [SMEM, VMEM, VMEM], [], 3, (place, *picked))


def correlate(place, flipped, full, inner, sink, copies):
    return call(
        correlate_kernel,
        "correlate",
        shape_of(F32, copies, 2, 128),
        [SMEM] + [VMEM] * 5,
        [],
        3,
        (place, flipped, full, *inner, sink),
    )


def swapped(value, axis, mask):
    count = lax.axis_size(axis)
    return lax.ppermute(value, axis, [(i, i ^ mask) for i in range(count)])


def shards(vectors, perambulators, shift_steps, spin_choice):
    vec = vectors[0]
    nvec = vec.shape[2]
    z_count, run_count = lax.axis_size("z"), lax.axis_size("z") * lax.axis_size("yl")
    space_count = run_count * lax.axis_size("core")
    combos = spin_choice.shape[0]
    factor = 1.0 / math.sqrt(24.0 * vec.shape[3] * space_count)
    corr_factor = 0.25 / (nvec * math.sqrt(nvec))
    core = lax.axis_index("core")
    run = lax.axis_index("z") * lax.axis_size("yl") + lax.axis_index("yl")
    peram = perambulators[0].reshape(-1, 2, nvec, nvec)

    beside = swapped(vec, "core", 1)
    part = pair_products(core[None], vec, factor)
    part = pair_products(core[None], beside, factor, part).reshape(run_count, -1, 128)
    time_count = lax.axis_size("yh") * lax.axis_size("x")
    now = lax.axis_index("yh") * lax.axis_size("x") + lax.axis_index("x")
    away_by = now ^ ((now + shift_steps[0]) % time_count)
    pick = (away_by & 1) * 4 + (away_by & 2) + (away_by >> 2)
    place = jnp.stack([core, run]).astype(jnp.int32)
    place, pick, part = lax.optimization_barrier((place, pick, part))
    spread = lax.all_to_all(part, ("z", "yl"), 0, 0, tiled=True)
    left_r, left_n, flipped, full = prepare(place, spin_choice, peram)
    spread, left_r = lax.optimization_barrier((spread, left_r))
    own, every = sum_parts(spread)

    one = swapped(own, "yh", 1)
    near = jnp.stack([own, one])
    two = swapped(near, "x", 2)
    wider = jnp.concatenate([near, two])
    four = swapped(wider, "x", 1)
    mine = lax.all_to_all(every, ("z", "yl"), 0, 0, tiled=True)
    mine = mine.reshape(-1, 128)
    theirs = swapped(mine, "core", 1)
    inner, picked = zip(first_index(0, left_r, left_n, mine), first_index(1, left_r, left_n, theirs), strict=True)
    four, inner = lax.optimization_barrier((four, inner))
    sink = lax.dynamic_index_in_dim(jnp.concatenate([wider, four]), pick, 0, keepdims=False)
    corr = correlate(place, flipped, full, inner, sink, space_count)
    total = lax.all_to_all(corr, ("z", "yl", "core"), 0, 0, tiled=True).sum(0)
    rows = own_rows(place, picked)
    correlator = jnp.transpose((total[:, :combos] * corr_factor)[None], (0, 2, 1))
    return (rows.reshape(1, 2, 2, nvec * nvec)[0], correlator)


def solution(mesh):
    fine = Mesh(mesh.devices.reshape(2, 4, 8, 2, 2), ("yh", "x", "z", "yl", "core"))
    times, space = ("yh", "x"), ("z", "yl", "core")
    placed = (P(times, None, None, None, space), P(times, None, None, None), P(times), P())

    def whole(vectors, perambulators, shift_steps, spin_choice):
        rows, correlator = shards(vectors, perambulators, shift_steps, spin_choice)
        return rows[None], correlator

    return jax.shard_map(
        whole,
        mesh=fine,
        in_specs=placed,
        out_specs=(P(times, space, None, None), P(times, None, None)),
        check_vma=False,
    )
```
